256 devices in a mesh: dp: 16 (over y, x_lo, core), head: 16 (over x_hi, z).
Axes of the slice: x: 4 (x_hi: 2, x_lo: 2; x = x_hi * 2 + x_lo), y: 4, z: 8, core: 2. Of those that a mesh axis runs over, the one named last changes fastest.
Arguments:
- latent: bfloat16 [16, 512, 3072], P('dp', None, 'head'), may hold values from -6 to 6
- noise: bfloat16 [16, 512, 3072], P('dp'), may hold values from -18 to 18
- steps: int32 [16], P('dp'), may hold values from 0 to 999
- gen_qkv: bfloat16 [3072, 6144], P(None, 'head'), may hold values from -0.109375 to 0.109375
- gen_out: bfloat16 [2048, 3072], P('head'), may hold values from -0.5 to 0.5
- real_qkv: bfloat16 [3072, 6144], P(None, 'head'), may hold values from -0.109375 to 0.109375
- real_out: bfloat16 [2048, 3072], P('head'), may hold values from -0.5 to 0.5
- fake_qkv: bfloat16 [3072, 6144], P('dp', 'head'), may hold values from -0.109375 to 0.109375
- fake_out: bfloat16 [3072, 2048], P('dp', 'head'), may hold values from -0.5 to 0.5
Outputs:
- score_grad: float32 [16, 512, 3072], P('dp', None, 'head')
- fake_qkv_grad: float32 [3072, 6144], P('dp', 'head')
- fake_out_grad: float32 [3072, 2048], P('dp', 'head')
The draws below stay inside these ranges and needn't reach their ends.
All inputs are finite; a program needn't handle non-finite values. Where the reference program divides by a largest or mean magnitude, that divisor is 1e-20 or more.
Results may differ from the reference program's by a relative error of at most 0.034.
Values may be sent and summed in bfloat16 or wider, within the bound.
No kernel may reach another device: no remote copies, remote signals or barrier semaphores. Data moves between devices by JAX's collectives and lax.ppermute only.
A program may use at most 128 MiB of HBM per device.

```python
import math
import jax
import jax.numpy as jnp
from jax import lax

D = 3072
HD = 128
L = 512
INNER = 2048
IMAGES = 16
N_HEAD = 16


def column_scales(low, ratio):
    column = jnp.arange(D, dtype=jnp.float32) / float(max(D - 1, 1))
    return low * jnp.power(ratio, column)


def draw_noise(key, part):
    key = jax.random.fold_in(key, 11)
    base = jax.random.normal(key, (IMAGES, L, D), jnp.float32)
    scaled = base * column_scales(0.5, 6.0)
    return jnp.clip(scaled, -18.0, 18.0).astype(jnp.bfloat16)


def touch_ends(result, rng, smallest, largest):
    place = [jax.random.randint(jax.random.fold_in(rng, axis), (), 0, length) for axis, length in enumerate(result.shape)]
    main_axis = result.shape.index(max(result.shape))
    neighbour = place[:main_axis] + [(place[main_axis] + 1) % result.shape[main_axis]] + place[main_axis + 1:]
    return result.at[tuple(place)].set(smallest).at[tuple(neighbour)].set(largest)


def shard_levels(key, dims, pieces, smallest, high):
    def one(position, shards_of):
        heights = jax.random.uniform(jax.random.fold_in(jax.random.fold_in(key, 6), position), (shards_of,), jnp.float32, smallest / len(pieces), high / len(pieces))
        return jnp.repeat(jnp.exp(heights), dims[position] // shards_of).reshape((-1,) + (1,) * (len(dims) - position - 1))

    gain = one(*pieces[0])
    for cut in pieces[1:]:
        gain = gain * one(*cut)
    return gain


def bell_draw(own_key, dims, scale, most, shards=(), kind=jnp.bfloat16):
    drawn = jax.random.normal(own_key, dims, jnp.float32) * scale
    if len(shards) > 0:
        drawn = shard_levels(own_key, dims, shards, -0.22, 0.18) * drawn
    return jnp.clip(drawn, min=-most, max=most).astype(kind)


def setup_inputs(seed: int = 0) -> dict:
    key_list = jax.random.split(jax.random.key(seed), 10)
    return {
        "latent": bell_draw(key_list[0], (IMAGES, L, D), 1.0, 6.0, ((0, 16), (2, 16))),
        "noise": draw_noise(jax.random.fold_in(key_list[9], 71), 0),
        "steps": touch_ends(jax.random.randint(key_list[2], (IMAGES,), 0, 1000), jax.random.fold_in(key_list[2], 1), 0, 999).astype(jnp.int32),
        "gen_qkv": bell_draw(key_list[3], (D, 3 * INNER), D ** -0.5, 0.109375, ((1, 16),)),
        "gen_out": bell_draw(key_list[4], (INNER, D), HD ** -0.5, 0.5, ((0, 16),)),
        "real_qkv": bell_draw(key_list[5], (D, 3 * INNER), D ** -0.5, 0.109375, ((1, 16),)),
        "real_out": bell_draw(key_list[6], (INNER, D), HD ** -0.5, 0.5, ((0, 16),)),
        "fake_qkv": bell_draw(key_list[7], (D, 3 * INNER), D ** -0.5, 0.109375, ((0, 16), (1, 16))),
        "fake_out": bell_draw(key_list[8], (D, INNER), HD ** -0.5, 0.5, ((0, 16), (1, 16))),
    }


highest = lax.Precision.HIGHEST

def layer_norm(values):
    floats = values.astype(jnp.float32)
    center = floats - lax.optimization_barrier(jnp.mean(floats, axis=-1, keepdims=True))
    spread = lax.optimization_barrier(jnp.mean(center * center, axis=-1, keepdims=True))
    return (center * lax.rsqrt(spread + 1e-06)).astype(jnp.bfloat16)

def noise_levels(step):
    angle = (step.astype(jnp.float32) + 1.0) / 1001.0 * (math.pi / 2.0)
    return (jnp.cos(angle), jnp.sin(angle))

def attend(packed):
    length = packed.shape[0]
    groups = packed.shape[1] // (3 * HD)
    split = packed.reshape(length, groups, 3, HD).astype(jnp.float32)
    query = split[:, :, 0]
    keys = split[:, :, 1]
    values = split[:, :, 2]
    scores = jnp.einsum('qge,kge->gqk', query, keys) / math.sqrt(HD)
    weights = jax.nn.softmax(scores, axis=-1)
    rounded = weights.astype(jnp.bfloat16)
    mixed = jnp.einsum('gqk,kge->qge', rounded.astype(jnp.float32), values)
    mixed = mixed.astype(jnp.bfloat16).reshape(length, groups * HD)
    return (weights, rounded, query, keys, values, mixed)

def attend_back(weights, rounded, query, keys, values, grad_mixed):
    length = grad_mixed.shape[0]
    groups = grad_mixed.shape[1] // HD
    upstream = grad_mixed.reshape(length, groups, HD)
    grad_values = jnp.einsum('gqk,qge->kge', rounded.astype(jnp.float32), upstream, precision=highest)
    grad_weights = jnp.einsum('qge,kge->gqk', upstream, values, precision=highest)
    inner = lax.optimization_barrier(jnp.sum(grad_weights * weights, axis=-1, keepdims=True))
    grad_scores = weights * (grad_weights - inner) / math.sqrt(HD)
    grad_query = jnp.einsum('gqk,kge->qge', grad_scores, keys, precision=highest)
    grad_keys = jnp.einsum('gqk,qge->kge', grad_scores, query, precision=highest)
    stacked = jnp.stack([grad_query, grad_keys, grad_values], axis=2)
    return stacked.reshape(length, groups * 3 * HD).astype(jnp.bfloat16)

def head_sum(mixed, weight_rows):
    length = mixed.shape[0]
    group_width = INNER // N_HEAD
    stacked = mixed.reshape(length, N_HEAD, group_width).transpose(1, 0, 2)
    blocks = weight_rows.reshape(N_HEAD, group_width, D)

    def add_group(total, pair):
        part = jnp.dot(pair[0], pair[1], preferred_element_type=jnp.float32)
        part = lax.optimization_barrier(part.astype(jnp.bfloat16)).astype(jnp.float32)
        return (total + part, None)
    total, _ = lax.scan(add_group, jnp.zeros((length, D), jnp.float32), (stacked, blocks))
    return total

def reference(latent, noise, steps, gen_qkv, gen_out, real_qkv, real_out, fake_qkv, fake_out):
    images = latent.shape[0]
    inv_root = 1.0 / math.sqrt(images * L)
    fake_rows = fake_out.T

    def one_image(carry, item):
        block, fresh, step = item
        gen_packed = jnp.dot(layer_norm(block), gen_qkv, preferred_element_type=jnp.float32).astype(jnp.bfloat16)
        gen_mixed = attend(gen_packed)[5]
        generated = (block.astype(jnp.float32) + head_sum(gen_mixed, gen_out)).astype(jnp.bfloat16)
        signal_scale, noise_scale = noise_levels(step)
        noised = (signal_scale * generated.astype(jnp.float32) + noise_scale * fresh.astype(jnp.float32)).astype(jnp.bfloat16)
        normed = layer_norm(noised)
        real_packed = jnp.dot(normed, real_qkv, preferred_element_type=jnp.float32).astype(jnp.bfloat16)
        real_eps = head_sum(attend(real_packed)[5], real_out)
        fake_packed = jnp.dot(normed, fake_qkv, preferred_element_type=jnp.float32).astype(jnp.bfloat16)
        weights, rounded, query, keys, values, fake_mixed = attend(fake_packed)
        fake_eps = head_sum(fake_mixed, fake_rows)
        gap = jnp.mean(jnp.abs(fresh.astype(jnp.float32) - real_eps))
        score_rows = (real_eps - fake_eps) / (gap + 1e-05)
        error = ((fake_eps - fresh.astype(jnp.float32)) * inv_root).astype(jnp.bfloat16)
        grad_mixed = jnp.dot(error, fake_out, preferred_element_type=jnp.float32)
        grad_packed = attend_back(weights, rounded, query, keys, values, grad_mixed)
        qkv_term = lax.dot_general(normed, grad_packed, (((0,), (0,)), ((), ())), preferred_element_type=jnp.float32)
        out_term = lax.dot_general(error, fake_mixed, (((0,), (0,)), ((), ())), preferred_element_type=jnp.float32)
        return ((carry[0] + qkv_term, carry[1] + out_term), score_rows)
    start = (jnp.zeros((D, 3 * INNER), jnp.float32), jnp.zeros((D, INNER), jnp.float32))
    grads, score_grad = lax.scan(one_image, start, (latent, noise, steps))
    return (score_grad, grads[0], grads[1])
```

```python
import math

import jax
import jax.numpy as jnp
from jax import lax
from jax.sharding import PartitionSpec as P

D = 3072
HD = 128
F = 192
BF = jnp.bfloat16
F32 = jnp.float32


def gather_head(block):
    return lax.all_gather(block, "head", axis=0, tiled=True)


def spread(block, axis):
    return lax.all_to_all(jnp.broadcast_to(block[None], (16,) + block.shape), axis, 0, 0)


def collect(parts, axis):
    got = lax.all_to_all(parts, axis, 0, 0)
    return jnp.sum(got.astype(F32), axis=0)


def layer_norm(values):
    floats = values.astype(F32)
    center = floats - jnp.mean(floats, axis=0, keepdims=True)
    spread = jnp.mean(center * center, axis=0, keepdims=True)
    return (center * lax.rsqrt(spread + 1e-06)).astype(BF)


def noise_levels(step):
    angle = (step.astype(F32) + 1.0) / 1001.0 * (math.pi / 2.0)
    return (jnp.cos(angle), jnp.sin(angle))


def dot(a, b, ca, cb):
    return lax.dot_general(a, b, (((ca,), (cb,)), ((), ())), preferred_element_type=F32)


def attend(packed):
    query, keys, values = packed[:, :HD], packed[:, HD : 2 * HD], packed[:, 2 * HD :]
    scores = dot(query, keys, 1, 1) / math.sqrt(HD)
    weights = jax.nn.softmax(scores, axis=-1)
    rounded = weights.astype(BF)
    mixed = dot(values, rounded, 0, 1).astype(BF)
    return weights, rounded, query, keys, values, mixed


def attend_back(weights, rounded, query, keys, values, grad_mixed):
    upstream = grad_mixed.astype(BF)
    grad_values = dot(rounded, upstream, 0, 0)
    grad_weights = dot(upstream, values, 1, 1)
    inner = jnp.sum(grad_weights * weights, axis=-1, keepdims=True)
    grad_scores = (weights * (grad_weights - inner) / math.sqrt(HD)).astype(BF)
    grad_query = dot(grad_scores, keys, 1, 0)
    grad_keys = dot(grad_scores, query, 0, 0)
    return jnp.concatenate([grad_query, grad_keys, grad_values], axis=1).astype(BF)


def local(latent, noise, steps, gen_qkv, gen_out, real_qkv, real_out, fake_qkv, fake_out):
    fresh = noise[0]
    length = fresh.shape[0]
    head = lax.axis_index("head")
    signal_scale, noise_scale = noise_levels(steps[0])
    inv_root = 1.0 / math.sqrt(length * lax.axis_size("dp"))
    fresh_cols = lax.dynamic_slice_in_dim(fresh, head * F, F, 1).T.astype(F32)

    def out_chunk(w):
        got = lax.all_to_all(w.reshape(16, F, HD), "head", 0, 0)
        return got.transpose(1, 0, 2).reshape(F, 16 * HD)

    tokens = latent[0].T
    whole = gather_head(tokens)
    gen_chunk = out_chunk(gen_out.T)
    fake_both = spread(jnp.concatenate([fake_qkv, fake_out], axis=1), "dp").reshape(D, 4 * HD)
    fake_full, fake_cols = fake_both[:, : 3 * HD], fake_both[:, 3 * HD :]
    fake_rows = spread(fake_out, "head").transpose(1, 0, 2).reshape(F, 16 * HD)
    fake_chunk = out_chunk(fake_cols)
    real_chunk = out_chunk(real_out.T)
    gram = collect(dot(fake_rows, fake_out, 0, 0).astype(BF).reshape(16, HD, HD), "dp")
    gram = spread(gram.astype(BF), "dp").reshape(16 * HD, HD)
    noise_back = dot(fresh, fake_cols, 1, 0)

    gen_packed = dot(layer_norm(whole), gen_qkv, 0, 0).astype(BF)
    gen_mixed = gather_head(attend(gen_packed)[5])
    branch = dot(gen_chunk, gen_mixed, 1, 0)
    generated = (tokens.astype(F32) + branch).astype(BF)
    noised_part = (signal_scale * generated.astype(F32) + noise_scale * fresh_cols).astype(BF)
    normed = layer_norm(gather_head(noised_part))

    fake_packed = dot(normed, fake_full, 0, 0).astype(BF)
    weights, rounded, query, keys, values, fake_mixed = attend(fake_packed)
    fake_all = gather_head(fake_mixed)
    real_packed = dot(normed, real_qkv, 0, 0).astype(BF)
    real_all = gather_head(attend(real_packed)[5])

    grad_mixed = inv_root * (dot(fake_all, gram, 0, 0) - noise_back)
    grad_packed = attend_back(weights, rounded, query, keys, values, grad_mixed)
    qkv_grad = dot(normed, grad_packed, 1, 0).astype(BF)
    fake_qkv_grad = collect(qkv_grad.reshape(16, F, 3 * HD), "dp")

    noise_term = dot(fresh, fake_mixed, 0, 1).astype(BF).reshape(16, F, HD)
    square = dot(fake_all, fake_mixed, 1, 1).astype(BF).reshape(16, HD, HD)
    summed = collect(jnp.concatenate([noise_term, square], axis=1), "dp")
    square_all = spread(summed[F:].astype(BF), "dp").reshape(16 * HD, HD)
    fake_out_grad = inv_root * (dot(fake_rows, square_all, 1, 0) - summed[:F])

    fake_eps = dot(fake_chunk, fake_all, 1, 0)
    real_eps = dot(real_chunk, real_all, 1, 0)
    gap_part = jnp.sum(jnp.abs(fresh_cols - real_eps))
    gap = jnp.sum(spread(jnp.full((1, HD), gap_part, F32), "head")[:, 0, 0]) / (length * D)
    score_grad = ((real_eps - fake_eps) / (gap + 1e-05)).T[None]
    return (score_grad, fake_qkv_grad, fake_out_grad)


def solution(mesh):
    in_specs = (
        P("dp", None, "head"),
        P("dp", None, None),
        P("dp"),
        P(None, "head"),
        P("head", None),
        P(None, "head"),
        P("head", None),
        P("dp", "head"),
        P("dp", "head"),
    )
    out_specs = (P("dp", None, "head"), P("dp", "head"), P("dp", "head"))
    return jax.shard_map(local, mesh=mesh, in_specs=in_specs, out_specs=out_specs, check_vma=False)
```

```python
import functools
import math

import jax
import jax.numpy as jnp
from jax import lax
from jax.experimental import pallas as pl
from jax.experimental.pallas import tpu as pltpu
from jax.sharding import PartitionSpec as P

D = 3072
HD = 128
L = 512
F = 192
Z = 8
INNER = 2048
BF = jnp.bfloat16
F32 = jnp.float32
ROOT = 1.0 / math.sqrt(HD)

HEAD = [(a, z) for a in range(2) for z in range(Z)]
ACROSS = [(a * Z + z, (1 - a) * Z + z) for a, z in HEAD]
TURN = [(i * 16 + h, h * 16 + i) for i in range(16) for h in range(16)]


def along(d):
    return [(a * Z + z, a * Z + (z + d) % Z) for a, z in HEAD]


def send(v, axis, pairs):
    return lax.ppermute(v, axis, pairs)


def ring(block, middle=None, *lead):
    def up(v):
        return send(v, "head", along(1))

    def down(v):
        return send(v, "head", along(-1))

    def across(v):
        return send(v, "head", ACROSS)

    own = [block] + [None] * 7
    other = [None] * 8
    other[0] = across(block)
    own[1], own[7] = down(block), up(block)
    done = ()
    if middle is not None:
        own[1], own[7], *lead = lax.optimization_barrier((own[1], own[7], *lead))
        done = middle(*lead)
    other[1], other[7] = across(own[1]), across(own[7])
    own[2], own[6] = down(own[1]), up(own[7])
    other[2], other[6] = down(other[1]), up(other[7])
    own[3], own[5] = down(own[2]), up(own[6])
    other[3], other[5] = down(other[2]), up(other[6])
    own[4] = down(own[3])
    other[4] = up(other[5])
    if done:
        own[4], other[4], *done = lax.optimization_barrier((own[4], other[4], *done))
    return own + other, done


def spread(block, axis):
    return lax.all_to_all(jnp.broadcast_to(block[None], (16,) + block.shape), axis, 0, 0)


def collect(parts, axis):
    got = lax.all_to_all(parts, axis, 0, 0)
    return jnp.sum(got.astype(F32), axis=0)


def noise_levels(step):
    angle = (step.astype(F32) + 1.0) / 1001.0 * (math.pi / 2.0)
    return (jnp.cos(angle), jnp.sin(angle))


def dot(a, b, ca, cb):
    return lax.dot_general(a, b, (((ca,), (cb,)), ((), ())), preferred_element_type=F32)


class Late:
    def __init__(self, source, target, semaphore):
        self.copy = pltpu.make_async_copy(source, target, semaphore)
        self.target = target
        self.waited = False
        self.copy.start()

    def __getitem__(self, index):
        if not self.waited:
            self.copy.wait()
            self.waited = True
        return self.target[index]


def run(body, outs, scalars, *arrays, scratch=(), flops=10**9):
    counts = [len(scalars), len(arrays), len(outs), len(arrays), len(scratch)]

    def kernel(*refs):
        groups, first = [], 0
        for count in counts:
            groups.append(refs[first : first + count])
            first += count
        numbers, sources, results, targets, spare = groups
        held = [Late(s, t, refs[-1].at[k]) for k, (s, t) in enumerate(zip(sources, targets))]
        body(*numbers, *held, *results, *spare)
        for late in held:
            if not late.waited:
                late.copy.wait()

    specs = [pl.BlockSpec(memory_space=pltpu.SMEM)] * len(scalars)
    specs += [pl.BlockSpec(memory_space=pl.ANY)] * len(arrays)
    return pl.pallas_call(
        kernel,
        out_shape=[jax.ShapeDtypeStruct(s, t) for s, t in outs],
        in_specs=specs,
        out_specs=[pl.BlockSpec(memory_space=pltpu.VMEM)] * len(outs),
        scratch_shapes=[
            *[pltpu.VMEM(v.shape, v.dtype) for v in arrays],
            *scratch,
            pltpu.SemaphoreType.DMA((len(arrays),)),
        ],
        compiler_params=pltpu.CompilerParams(vmem_limit_bytes=56 * 1024 * 1024),
        cost_estimate=pl.CostEstimate(flops=flops, bytes_accessed=8 * 2**20, transcendentals=0),
    )(*scalars, *arrays)


def softmax_attend(packed):
    query = packed[:HD].T
    keys, values = packed[HD : 2 * HD], packed[2 * HD :]
    scores = dot(query, keys, 1, 0) * ROOT
    powers = jnp.exp(scores - jnp.max(scores, axis=1, keepdims=True))
    weights = powers / jnp.sum(powers, axis=1, keepdims=True)
    mixed = dot(values, weights.astype(BF), 1, 1).astype(BF)
    return weights, mixed


def normalize(place, blocks, normed):
    total = jnp.zeros((8, L), F32)
    for b in blocks:
        total = total + jnp.sum(b[:, :L].astype(F32).reshape(F // 8, 8, L), axis=0)
    mean = jnp.sum(total, axis=0, keepdims=True) / D
    total = jnp.zeros((8, L), F32)
    for b in blocks:
        center = b[:, :L].astype(F32) - mean
        total = total + jnp.sum((center * center).reshape(F // 8, 8, L), axis=0)
    scale = lax.rsqrt(jnp.sum(total, axis=0, keepdims=True) / D + 1e-06)
    for k, b in enumerate(blocks):
        rows = pl.ds(pl.multiple_of(place[k] * F, F), F)
        normed[rows, :] = ((b[:, :L].astype(F32) - mean) * scale).astype(BF)


def gather_slices(place, blocks, first, whole):
    for k, b in enumerate(blocks):
        for s in range(8):
            rows = pl.ds(pl.multiple_of(place[k] * 16 + s * 256, 16), 16)
            whole[rows, :] = b[first + s * 16 : first + s * 16 + 16, :]


def project_slices(which, weights, whole):
    total = jnp.zeros((F, L), F32)
    for s in range(8):
        weight = weights[2 * s + which, :, HD:]
        total = total + dot(weight, whole[s * 256 : (s + 1) * 256, :], 1, 0)
    return total


def gen_body(place, *refs):
    blocks, (weight, mixed, fake_rows, gram, normed) = refs[:16], refs[16:]
    normalize(place, blocks, normed)
    packed = dot(weight[...].T, normed[...], 1, 0).astype(BF)
    mixed[...] = softmax_attend(packed)[1]
    mine = blocks[0][:, L:].T
    for k, b in enumerate(blocks):
        part = b[:, L:]
        fake_rows[:, pl.ds(pl.multiple_of(place[k] * HD, HD), HD)] = part
        gram[place[k]] = dot(mine, part, 1, 0).astype(BF)


def noise_back_body(weights, fresh, noise_back):
    columns = jnp.concatenate([weights[i, :, :HD] for i in range(16)], axis=0).T
    noise_back[...] = dot(columns, fresh[...], 1, 1)


def fake_body(place, *refs):
    blocks, (weight, mixed, packed, weights, normed) = refs[:16], refs[16:]
    normalize(place, blocks, normed)
    packed[...] = dot(weight[...].T, normed[...], 1, 0).astype(BF)
    weights[...], mixed[...] = softmax_attend(packed[...])


def real_body(normed, weight, fresh, fake_mixed, mixed, noise_term):
    packed = dot(weight[...].T, normed[...], 1, 0).astype(BF)
    mixed[...] = softmax_attend(packed)[1]
    term = dot(fresh[...].T, fake_mixed[...], 1, 1).astype(BF)
    noise_term[...] = term.reshape(16, F, HD)


def noised_body(place, levels, *refs):
    blocks, (weights, tokens, fresh, noised, whole) = refs[:16], refs[16:]
    gather_slices(place, blocks, 0, whole)
    branch = project_slices(0, weights, whole)
    generated = (tokens[...].astype(F32) + branch).astype(BF)
    noised[...] = (
        levels[0] * generated.astype(F32) + levels[1] * fresh[...].astype(F32)
    ).astype(BF)


def back_body(inv_root, place, *refs):
    blocks, refs = refs[:16], refs[16:]
    gram, noise_back, packed, weights, mine, normed, grad, whole = refs
    for k, b in enumerate(blocks):
        whole[pl.ds(pl.multiple_of(place[k] * HD, HD), HD), :] = b[...]
    back = jnp.concatenate([gram[g] for g in range(16)], axis=1)
    upstream = inv_root * (dot(back, whole[...], 1, 0) - noise_back[...])
    upstream = upstream.astype(BF)
    held = packed[...]
    query, keys, values = held[:HD], held[HD : 2 * HD], held[2 * HD :]
    chances = weights[...]
    grad_weights = dot(upstream.T, values, 1, 0)
    inner = jnp.sum(grad_weights * chances, axis=1, keepdims=True)
    grad_scores = (chances * (grad_weights - inner) * ROOT).astype(BF)
    grad_values = dot(upstream, chances.astype(BF), 1, 0)
    grad_query = dot(keys, grad_scores, 1, 1)
    grad_keys = dot(query, grad_scores, 1, 0)
    for n, part in enumerate((grad_query, grad_keys, grad_values)):
        rows = dot(normed[...], part.astype(BF), 1, 1).astype(BF)
        grad[:, n * F : (n + 1) * F, :] = rows.reshape(16, F, HD)
    square = dot(whole[...], mine[...], 1, 1).astype(BF)
    grad[:, 3 * F :, :] = square.reshape(16, HD, HD)


def score_body(place, *refs):
    real, fake, refs = refs[:16], refs[16:32], refs[32:]
    weights, fake_chunk, fresh, gap, diff, whole = refs
    gather_slices(place, real, 0, whole)
    real_eps = project_slices(1, weights, whole)
    part = jnp.sum(jnp.abs(fresh[...].astype(F32) - real_eps))
    gap[...] = jnp.full((8, HD), part, F32)
    for k, b in enumerate(fake):
        whole[pl.ds(pl.multiple_of(place[k] * HD, HD), HD), :] = b[...]
    fake_eps = dot(fake_chunk[...], whole[...], 1, 0)
    diff[...] = (real_eps - fake_eps).T


def out_body(inv_root, rows, square, noise, grad):
    total = jnp.zeros((F, HD), F32)
    for g in range(16):
        total = total + dot(rows[:, g * HD : (g + 1) * HD], square[g], 1, 0)
    grad[...] = inv_root * (total - noise[...])


def local(latent, noise, steps, gen_qkv, gen_out, real_qkv, real_out, fake_qkv, fake_out):
    fresh = noise[0]
    head = lax.axis_index("head")
    dp = lax.axis_index("dp")
    a, z = head // Z, head % Z
    offsets = (z + jnp.arange(Z)) % Z
    place = jnp.concatenate([a * Z + offsets, (1 - a) * Z + offsets]).astype(jnp.int32)
    levels = jnp.stack(noise_levels(steps[0]))
    inv_root = 1.0 / math.sqrt(L * 16)
    fresh_cols = lax.dynamic_slice_in_dim(fresh, head * F, F, 1).T

    start = dp // 2 * 16
    rows = jnp.where(
        dp % 2 == 0,
        lax.dynamic_slice_in_dim(gen_out, start, 16, 0),
        lax.dynamic_slice_in_dim(real_out, start, 16, 0),
    )
    rows = rows.reshape(16, 16, F).transpose(1, 0, 2)

    def exchange_rows(v):
        return (lax.all_to_all(v, "head", 0, 0),)

    tokens = latent[0].T
    blocks, (rows,) = ring(jnp.concatenate([tokens, fake_out], axis=1), exchange_rows, rows)
    rows = rows.reshape(256, F).T
    fake_full = lax.all_gather(fake_qkv, "dp", axis=0, tiled=True)
    weights = lax.all_gather(jnp.concatenate([fake_out, rows], axis=1), "dp", axis=0)

    gen_mixed, fake_rows, gram = run(
        gen_body,
        [((HD, L), BF), ((F, INNER), BF), ((16, HD, HD), BF)],
        [place],
        *blocks,
        gen_qkv,
        scratch=[pltpu.VMEM((D, L), BF)],
    )

    def sum_gram(v):
        return (collect(v, "dp").astype(BF),)

    gen_blocks, (gram,) = ring(gen_mixed, sum_gram, gram)
    (noised_part,) = run(
        noised_body,
        [((F, L), BF)],
        [place, levels],
        *gen_blocks,
        weights,
        tokens,
        fresh_cols,
        scratch=[pltpu.VMEM((INNER, L), BF)],
    )

    def spread_gram(v, weights, fresh):
        return (spread(v, "dp"), *run(noise_back_body, [((HD, L), F32)], [], weights, fresh))

    noised, (gram, noise_back) = ring(noised_part, spread_gram, gram, weights, fresh)
    fake_mixed, packed, chances, normed = run(
        fake_body,
        [((HD, L), BF), ((3 * HD, L), BF), ((L, L), F32), ((D, L), BF)],
        [place],
        *noised,
        fake_full,
    )

    def real_and_noise(*v):
        real_mixed, term = run(real_body, [((HD, L), BF), ((16, F, HD), BF)], [], *v)
        return real_mixed, collect(term, "dp")

    fake_blocks, (real_mixed, noise_term) = ring(
        fake_mixed, real_and_noise, normed, real_qkv, fresh, fake_mixed
    )
    fake_blocks[15], fake_rows = lax.optimization_barrier((fake_blocks[15], fake_rows))
    fake_chunk = send(fake_rows, ("dp", "head"), TURN)
    (grad,) = run(
        functools.partial(back_body, inv_root),
        [((16, 3 * F + HD, HD), BF)],
        [place],
        *fake_blocks,
        gram,
        noise_back,
        packed,
        chances,
        fake_mixed,
        normed,
        scratch=[pltpu.VMEM((INNER, L), BF)],
    )
    grad, real_mixed = lax.optimization_barrier((grad, real_mixed))
    got = lax.all_to_all(grad, "dp", 0, 0)
    real_blocks, _ = ring(real_mixed)
    square = jnp.sum(got[:, 3 * F :].astype(F32), axis=0).astype(BF)
    fake_qkv_grad = jnp.concatenate(
        [jnp.sum(got[:, n * F : (n + 1) * F].astype(F32), axis=0) for n in range(3)], axis=1
    )
    (fake_out_grad,) = run(
        functools.partial(out_body, inv_root),
        [((F, HD), F32)],
        [],
        fake_rows,
        spread(square, "dp"),
        noise_term,
    )

    gap, diff = run(
        score_body,
        [((8, HD), F32), ((L, F), F32)],
        [place],
        *real_blocks,
        *fake_blocks,
        weights,
        fake_chunk,
        fresh_cols,
        scratch=[pltpu.VMEM((INNER, L), BF)],
    )
    gap = jnp.sum(spread(gap, "head")[:, 0, 0]) / (L * D)
    score_grad = (diff / (gap + 1e-05))[None]
    return (score_grad, fake_qkv_grad, fake_out_grad)


def solution(mesh):
    in_specs = (
        P("dp", None, "head"),
        P("dp", None, None),
        P("dp"),
        P(None, "head"),
        P("head", None),
        P(None, "head"),
        P("head", None),
        P("dp", "head"),
        P("dp", "head"),
    )
    out_specs = (P("dp", None, "head"), P("dp", "head"), P("dp", "head"))
    return jax.shard_map(local, mesh=mesh, in_specs=in_specs, out_specs=out_specs, check_vma=False)
```

```python
import functools
import math

import jax
import jax.numpy as jnp
from jax import lax
from jax.experimental import pallas as pl
from jax.experimental.pallas import tpu as pltpu
from jax.sharding import PartitionSpec as P

D = 3072
HD = 128
L = 512
F = 192
Z = 8
INNER = 2048
BF = jnp.bfloat16
F32 = jnp.float32
ROOT = 1.0 / math.sqrt(HD)

HEAD = [(a, z) for a in range(2) for z in range(Z)]
ACROSS = [(a * Z + z, (1 - a) * Z + z) for a, z in HEAD]


def along(d):
    return [(a * Z + z, a * Z + (z + d) % Z) for a, z in HEAD]


def send(v, axis, pairs):
    return lax.ppermute(v, axis, pairs)


def ring(block):
    def up(v):
        return send(v, "head", along(1))

    def down(v):
        return send(v, "head", along(-1))

    def across(v):
        return send(v, "head", ACROSS)

    own = [block] + [None] * 7
    other = [None] * 8
    other[0] = across(block)
    own[1], own[7] = down(block), up(block)
    other[1], other[7] = across(own[1]), across(own[7])
    own[2], own[6] = down(own[1]), up(own[7])
    other[2], other[6] = down(other[1]), up(other[7])
    own[3], own[5] = down(own[2]), up(own[6])
    other[3], other[5] = down(other[2]), up(other[6])
    own[4] = down(own[3])
    other[4] = up(other[5])
    return own + other


def join(blocks, *arrays):
    blocks[4], blocks[12], *arrays = lax.optimization_barrier((blocks[4], blocks[12], *arrays))
    return arrays


def spread(block, axis):
    return lax.all_to_all(jnp.broadcast_to(block[None], (16,) + block.shape), axis, 0, 0)


def collect(parts, axis):
    got = lax.all_to_all(parts, axis, 0, 0)
    return jnp.sum(got.astype(F32), axis=0)


def noise_levels(step):
    angle = (step.astype(F32) + 1.0) / 1001.0 * (math.pi / 2.0)
    return (jnp.cos(angle), jnp.sin(angle))


def dot(a, b, ca, cb):
    return lax.dot_general(a, b, (((ca,), (cb,)), ((), ())), preferred_element_type=F32)


class Late:
    def __init__(self, source, target, semaphore):
        self.copy = pltpu.make_async_copy(source, target, semaphore)
        self.target = target
        self.waited = False
        self.copy.start()

    def __getitem__(self, index):
        if not self.waited:
            self.copy.wait()
            self.waited = True
        return self.target[index]


def run(body, outs, scalars, *arrays, scratch=(), flops=10**9):
    counts = [len(scalars), len(arrays), len(outs), len(arrays), len(scratch)]

    def kernel(*refs):
        groups, first = [], 0
        for count in counts:
            groups.append(refs[first : first + count])
            first += count
        numbers, sources, results, targets, spare = groups
        held = [Late(s, t, refs[-1].at[k]) for k, (s, t) in enumerate(zip(sources, targets))]
        body(*numbers, *held, *results, *spare)
        for late in held:
            if not late.waited:
                late.copy.wait()

    specs = [pl.BlockSpec(memory_space=pltpu.SMEM)] * len(scalars)
    specs += [pl.BlockSpec(memory_space=pl.ANY)] * len(arrays)
    return pl.pallas_call(
        kernel,
        out_shape=[jax.ShapeDtypeStruct(s, t) for s, t in outs],
        in_specs=specs,
        out_specs=[pl.BlockSpec(memory_space=pltpu.VMEM)] * len(outs),
        scratch_shapes=[
            *[pltpu.VMEM(v.shape, v.dtype) for v in arrays],
            *scratch,
            pltpu.SemaphoreType.DMA((len(arrays),)),
        ],
        compiler_params=pltpu.CompilerParams(vmem_limit_bytes=56 * 1024 * 1024),
        cost_estimate=pl.CostEstimate(flops=flops, bytes_accessed=8 * 2**20, transcendentals=0),
    )(*scalars, *arrays)


def softmax_attend(packed):
    query = packed[:HD].T
    keys, values = packed[HD : 2 * HD], packed[2 * HD :]
    scores = dot(query, keys, 1, 0) * ROOT
    powers = jnp.exp(scores - jnp.max(scores, axis=1, keepdims=True))
    weights = powers / jnp.sum(powers, axis=1, keepdims=True)
    mixed = dot(values, weights.astype(BF), 1, 1).astype(BF)
    return weights, mixed


def normalize(place, blocks, normed):
    total = jnp.zeros((8, L), F32)
    for b in blocks:
        total = total + jnp.sum(b[:, :L].astype(F32).reshape(F // 8, 8, L), axis=0)
    mean = jnp.sum(total, axis=0, keepdims=True) / D
    total = jnp.zeros((8, L), F32)
    for b in blocks:
        center = b[:, :L].astype(F32) - mean
        total = total + jnp.sum((center * center).reshape(F // 8, 8, L), axis=0)
    scale = lax.rsqrt(jnp.sum(total, axis=0, keepdims=True) / D + 1e-06)
    for k, b in enumerate(blocks):
        rows = pl.ds(pl.multiple_of(place[k] * F, F), F)
        normed[rows, :] = ((b[:, :L].astype(F32) - mean) * scale).astype(BF)


def gather_slices(place, blocks, first, whole):
    for k, b in enumerate(blocks):
        for s in range(8):
            rows = pl.ds(pl.multiple_of(place[k] * 16 + s * 256, 16), 16)
            whole[rows, :] = b[first + s * 16 : first + s * 16 + 16, :]


def project_slices(which, weights, whole):
    total = jnp.zeros((F, L), F32)
    for s in range(8):
        weight = weights[2 * s + which, :, HD:]
        total = total + dot(weight, whole[s * 256 : (s + 1) * 256, :], 1, 0)
    return total


def gen_body(place, *refs):
    blocks, (weight, mixed, fake_rows, gram, normed) = refs[:16], refs[16:]
    normalize(place, blocks, normed)
    packed = dot(weight[...].T, normed[...], 1, 0).astype(BF)
    mixed[...] = softmax_attend(packed)[1]
    mine = blocks[0][:, L:].T
    for k, b in enumerate(blocks):
        part = b[:, L:]
        fake_rows[:, pl.ds(pl.multiple_of(place[k] * HD, HD), HD)] = part
        gram[place[k]] = dot(mine, part, 1, 0).astype(BF)


def both_body(place, *refs):
    blocks, refs = refs[:16], refs[16:]
    fake_weight, real_weight, mixed, packed, weights, normed = refs
    normalize(place, blocks, normed)
    packed[...] = dot(fake_weight[...].T, normed[...], 1, 0).astype(BF)
    weights[...], mixed[:HD, :] = softmax_attend(packed[...])
    real_packed = dot(real_weight[...].T, normed[...], 1, 0).astype(BF)
    mixed[HD:, :] = softmax_attend(real_packed)[1]


def noised_body(place, levels, *refs):
    blocks, (weights, tokens, fresh, noised, whole) = refs[:16], refs[16:]
    gather_slices(place, blocks, 0, whole)
    branch = project_slices(0, weights, whole)
    generated = (tokens[...].astype(F32) + branch).astype(BF)
    noised[...] = (
        levels[0] * generated.astype(F32) + levels[1] * fresh[...].astype(F32)
    ).astype(BF)


def back_body(inv_root, place, *refs):
    blocks, refs = refs[:16], refs[16:]
    gram, noise_back, packed, weights, mine, normed, grad, whole = refs
    for k, b in enumerate(blocks):
        whole[pl.ds(pl.multiple_of(place[k] * HD, HD), HD), :] = b[:HD, :]
    back = jnp.concatenate([gram[g] for g in range(16)], axis=1)
    upstream = inv_root * (dot(back, whole[...], 1, 0) - noise_back[...])
    upstream = upstream.astype(BF)
    held = packed[...]
    query, keys, values = held[:HD], held[HD : 2 * HD], held[2 * HD :]
    chances = weights[...]
    grad_weights = dot(upstream.T, values, 1, 0)
    inner = jnp.sum(grad_weights * chances, axis=1, keepdims=True)
    grad_scores = (chances * (grad_weights - inner) * ROOT).astype(BF)
    grad_values = dot(upstream, chances.astype(BF), 1, 0)
    grad_query = dot(keys, grad_scores, 1, 1)
    grad_keys = dot(query, grad_scores, 1, 0)
    grad_packed = jnp.concatenate([grad_query, grad_keys, grad_values], axis=0).astype(BF)
    rows = dot(normed[...], grad_packed, 1, 1).astype(BF)
    for n in range(3):
        grad[:, n * F : (n + 1) * F, :] = rows[:, n * HD : (n + 1) * HD].reshape(16, F, HD)
    square = dot(whole[...], mine[:HD, :], 1, 1).astype(BF)
    grad[:, 3 * F :, :] = square.reshape(16, HD, HD)


def score_body(place, *refs):
    blocks, refs = refs[:16], refs[16:]
    weights, fake_chunk, fresh, gap, diff, whole = refs
    gather_slices(place, blocks, HD, whole)
    real_eps = project_slices(1, weights, whole)
    part = jnp.sum(jnp.abs(fresh[...].astype(F32) - real_eps))
    gap[...] = jnp.full((8, HD), part, F32)
    for k, b in enumerate(blocks):
        whole[pl.ds(pl.multiple_of(place[k] * HD, HD), HD), :] = b[:HD, :]
    chunk = jnp.concatenate([fake_chunk[g] for g in range(16)], axis=1)
    fake_eps = dot(chunk, whole[...], 1, 0)
    diff[...] = (real_eps - fake_eps).T


def out_body(inv_root, rows, square, noise, grad):
    total = jnp.zeros((F, HD), F32)
    for g in range(16):
        total = total + dot(rows[:, g * HD : (g + 1) * HD], square[g], 1, 0)
    grad[...] = inv_root * (total - noise[...])


def local(latent, noise, steps, gen_qkv, gen_out, real_qkv, real_out, fake_qkv, fake_out):
    fresh = noise[0]
    head = lax.axis_index("head")
    dp = lax.axis_index("dp")
    a, z = head // Z, head % Z
    offsets = (z + jnp.arange(Z)) % Z
    place = jnp.concatenate([a * Z + offsets, (1 - a) * Z + offsets]).astype(jnp.int32)
    levels = jnp.stack(noise_levels(steps[0]))
    inv_root = 1.0 / math.sqrt(L * 16)
    fresh_cols = lax.dynamic_slice_in_dim(fresh, head * F, F, 1).T

    start = dp // 2 * 16
    rows = jnp.where(
        dp % 2 == 0,
        lax.dynamic_slice_in_dim(gen_out, start, 16, 0),
        lax.dynamic_slice_in_dim(real_out, start, 16, 0),
    )
    rows = rows.reshape(16, 16, F).transpose(1, 0, 2)

    rows = lax.all_to_all(rows, "head", 0, 0)
    tokens = latent[0].T
    blocks = ring(jnp.concatenate([tokens, fake_out], axis=1))
    gen_mixed, fake_rows, gram = run(
        gen_body,
        [((HD, L), BF), ((F, INNER), BF), ((16, HD, HD), BF)],
        [place],
        *blocks,
        gen_qkv,
        scratch=[pltpu.VMEM((D, L), BF)],
    )
    gen_mixed, rows = lax.optimization_barrier((gen_mixed, rows))
    rows = rows.reshape(256, F).T
    fake_full = lax.all_gather(fake_qkv, "dp", axis=0, tiled=True)
    weights = lax.all_gather(jnp.concatenate([fake_out, rows], axis=1), "dp", axis=0)

    gram = collect(gram, "dp").astype(BF)
    blocks = ring(gen_mixed)
    (gram,) = join(blocks, gram)
    (noised_part,) = run(
        noised_body,
        [((F, L), BF)],
        [place, levels],
        *blocks,
        weights,
        tokens,
        fresh_cols,
        scratch=[pltpu.VMEM((INNER, L), BF)],
    )
    gram = lax.all_gather(jnp.pad(gram, ((0, F - HD), (0, 2 * HD))), "dp", axis=0)
    gram = gram[:, :HD, :HD]

    blocks = ring(noised_part)
    fake_cols = weights[:, :, :HD]
    (fake_cols,) = join(blocks, fake_cols)
    fake_chunk = lax.all_to_all(fake_cols, "head", 0, 0)
    mixed, packed, chances, normed = run(
        both_body,
        [((2 * HD, L), BF), ((3 * HD, L), BF), ((L, L), F32), ((D, L), BF)],
        [place],
        *blocks,
        fake_full,
        real_qkv,
    )
    blocks = ring(mixed)
    noise_back = dot(fake_cols.reshape(D, HD), fresh, 0, 1)
    noise_term = dot(fresh, mixed[:HD], 0, 1).astype(BF)
    fake_chunk, noise_back, noise_term = join(blocks, fake_chunk, noise_back, noise_term)
    noise_term = lax.psum_scatter(noise_term, "dp", scatter_dimension=0, tiled=True).astype(F32)
    (grad,) = run(
        functools.partial(back_body, inv_root),
        [((16, 3 * F + HD, HD), BF)],
        [place],
        *blocks,
        gram,
        noise_back,
        packed,
        chances,
        mixed,
        normed,
        scratch=[pltpu.VMEM((INNER, L), BF)],
    )
    grad, weights = lax.optimization_barrier((grad, weights))
    got = lax.all_to_all(grad, "dp", 0, 0)
    gap, diff = run(
        score_body,
        [((8, HD), F32), ((L, F), F32)],
        [place],
        *blocks,
        weights,
        fake_chunk,
        fresh_cols,
        scratch=[pltpu.VMEM((INNER, L), BF)],
    )
    for d in (1, 2, 4):
        gap = gap + send(gap, "head", along(d))
    gap = gap + send(gap, "head", ACROSS)
    score_grad = (diff / (gap[0, 0] / (L * D) + 1e-05))[None]

    square = jnp.sum(got[:, 3 * F :].astype(F32), axis=0).astype(BF)
    fake_qkv_grad = jnp.concatenate(
        [jnp.sum(got[:, n * F : (n + 1) * F].astype(F32), axis=0) for n in range(3)], axis=1
    )
    (fake_out_grad,) = run(
        functools.partial(out_body, inv_root),
        [((F, HD), F32)],
        [],
        fake_rows,
        spread(square, "dp"),
        noise_term,
    )
    return (score_grad, fake_qkv_grad, fake_out_grad)


def solution(mesh):
    in_specs = (
        P("dp", None, "head"),
        P("dp", None, None),
        P("dp"),
        P(None, "head"),
        P("head", None),
        P(None, "head"),
        P("head", None),
        P("dp", "head"),
        P("dp", "head"),
    )
    out_specs = (P("dp", None, "head"), P("dp", "head"), P("dp", "head"))
    return jax.shard_map(local, mesh=mesh, in_specs=in_specs, out_specs=out_specs, check_vma=False)
```

```python
import functools
import math

import jax
import jax.numpy as jnp
from jax import lax
from jax.experimental import pallas as pl
from jax.experimental.pallas import tpu as pltpu
from jax.sharding import PartitionSpec as P

D = 3072
HD = 128
L = 512
F = 192
Z = 8
INNER = 2048
BF = jnp.bfloat16
F32 = jnp.float32
ROOT = 1.0 / math.sqrt(HD)

HEAD = [(a, z) for a in range(2) for z in range(Z)]
ACROSS = [(a * Z + z, (1 - a) * Z + z) for a, z in HEAD]


def along(d):
    return [(a * Z + z, a * Z + (z + d) % Z) for a, z in HEAD]


def send(v, axis, pairs):
    return lax.ppermute(v, axis, pairs)


def ring(block):
    def up(v):
        return send(v, "head", along(1))

    def down(v):
        return send(v, "head", along(-1))

    def across(v):
        return send(v, "head", ACROSS)

    own = [block] + [None] * 7
    other = [None] * 8
    other[0] = across(block)
    own[1], own[7] = down(block), up(block)
    own[2], own[6] = down(own[1]), up(own[7])
    other[1], other[7] = down(other[0]), up(other[0])
    other[2], other[6] = down(other[1]), up(other[7])
    own[3], own[5] = down(own[2]), up(own[6])
    other[3], other[5] = down(other[2]), up(other[6])
    own[4] = down(own[3])
    other[4] = up(other[5])
    return own + other


def join(blocks, *arrays):
    blocks[4], blocks[12], *arrays = lax.optimization_barrier((blocks[4], blocks[12], *arrays))
    return arrays


def spread(block, axis):
    return lax.all_to_all(jnp.broadcast_to(block[None], (16,) + block.shape), axis, 0, 0)


def collect(parts, axis):
    got = lax.all_to_all(parts, axis, 0, 0)
    return jnp.sum(got.astype(F32), axis=0)


def noise_levels(step):
    angle = (step.astype(F32) + 1.0) / 1001.0 * (math.pi / 2.0)
    return (jnp.cos(angle), jnp.sin(angle))


def dot(a, b, ca, cb):
    return lax.dot_general(a, b, (((ca,), (cb,)), ((), ())), preferred_element_type=F32)


class Late:
    def __init__(self, source, target, semaphore):
        self.copy = pltpu.make_async_copy(source, target, semaphore)
        self.target = target
        self.waited = False
        self.copy.start()

    def __getitem__(self, index):
        if not self.waited:
            self.copy.wait()
            self.waited = True
        return self.target[index]


def run(body, outs, scalars, *arrays, scratch=(), flops=10**9):
    cuts = [v[1] if isinstance(v, tuple) else None for v in arrays]
    arrays = [v[0] if isinstance(v, tuple) else v for v in arrays]
    shapes = [
        v.shape if c is None else tuple(s.stop - s.start for s in c)
        for v, c in zip(arrays, cuts)
    ]
    counts = [len(scalars), len(arrays), len(outs), len(arrays), len(scratch)]

    def kernel(*refs):
        groups, first = [], 0
        for count in counts:
            groups.append(refs[first : first + count])
            first += count
        numbers, sources, results, targets, spare = groups
        sources = [s if c is None else s.at[c] for s, c in zip(sources, cuts)]
        held = [Late(s, t, refs[-1].at[k]) for k, (s, t) in enumerate(zip(sources, targets))]
        body(*numbers, *held, *results, *spare)
        for late in held:
            if not late.waited:
                late.copy.wait()

    specs = [pl.BlockSpec(memory_space=pltpu.SMEM)] * len(scalars)
    specs += [pl.BlockSpec(memory_space=pl.ANY)] * len(arrays)
    return pl.pallas_call(
        kernel,
        out_shape=[jax.ShapeDtypeStruct(s, t) for s, t in outs],
        in_specs=specs,
        out_specs=[pl.BlockSpec(memory_space=pltpu.VMEM)] * len(outs),
        scratch_shapes=[
            *[pltpu.VMEM(s, v.dtype) for s, v in zip(shapes, arrays)],
            *scratch,
            pltpu.SemaphoreType.DMA((len(arrays),)),
        ],
        compiler_params=pltpu.CompilerParams(vmem_limit_bytes=56 * 1024 * 1024),
        cost_estimate=pl.CostEstimate(flops=flops, bytes_accessed=8 * 2**20, transcendentals=0),
    )(*scalars, *arrays)


def softmax_attend(packed):
    query = packed[:HD].T
    keys, values = packed[HD : 2 * HD], packed[2 * HD :]
    scores = dot(query, keys, 1, 0) * ROOT
    powers = jnp.exp(scores - jnp.max(scores, axis=1, keepdims=True))
    weights = powers / jnp.sum(powers, axis=1, keepdims=True)
    mixed = dot(values, weights.astype(BF), 1, 1).astype(BF)
    return weights, mixed


def normalize(place, blocks, normed):
    total = jnp.zeros((8, L), F32)
    for b in blocks:
        total = total + jnp.sum(b[:, :L].astype(F32).reshape(F // 8, 8, L), axis=0)
    mean = jnp.sum(total, axis=0, keepdims=True) / D
    total = jnp.zeros((8, L), F32)
    for b in blocks:
        center = b[:, :L].astype(F32) - mean
        total = total + jnp.sum((center * center).reshape(F // 8, 8, L), axis=0)
    scale = lax.rsqrt(jnp.sum(total, axis=0, keepdims=True) / D + 1e-06)
    for k, b in enumerate(blocks):
        rows = pl.ds(pl.multiple_of(place[k] * F, F), F)
        normed[rows, :] = ((b[:, :L].astype(F32) - mean) * scale).astype(BF)


def gather_slices(place, blocks, first, whole):
    for k, b in enumerate(blocks):
        for s in range(8):
            rows = pl.ds(pl.multiple_of(place[k] * 16 + s * 256, 16), 16)
            whole[rows, :] = b[first + s * 16 : first + s * 16 + 16, :]


def project_slices(which, weights, whole):
    total = jnp.zeros((F, L), F32)
    for s in range(8):
        weight = weights[2 * s + which, :, HD:]
        total = total + dot(weight, whole[s * 256 : (s + 1) * 256, :], 1, 0)
    return total


def gen_body(place, *refs):
    blocks, (weight, mixed, fake_rows, gram, normed) = refs[:16], refs[16:]
    normalize(place, blocks, normed)
    packed = dot(weight[...].T, normed[...], 1, 0).astype(BF)
    mixed[...] = softmax_attend(packed)[1]
    mine = blocks[0][:, L:].T
    for k, b in enumerate(blocks):
        part = b[:, L:]
        fake_rows[:, pl.ds(pl.multiple_of(place[k] * HD, HD), HD)] = part
        gram[place[k], :HD, :] = dot(mine, part, 1, 0).astype(BF)
        gram[place[k], HD:, :] = jnp.zeros((F - HD, HD), BF)


def both_body(place, *refs):
    blocks, refs = refs[:16], refs[16:]
    fake_weight, real_weight, mixed, packed, weights, normed = refs
    normalize(place, blocks, normed)
    packed[...] = dot(fake_weight[...].T, normed[...], 1, 0).astype(BF)
    weights[...], mixed[:HD, :] = softmax_attend(packed[...])
    real_packed = dot(real_weight[...].T, normed[...], 1, 0).astype(BF)
    mixed[HD:, :] = softmax_attend(real_packed)[1]


def noised_body(place, levels, *refs):
    blocks, (weights, tokens, fresh, noised, columns, whole) = refs[:16], refs[16:]
    gather_slices(place, blocks, 0, whole)
    branch = project_slices(0, weights, whole)
    generated = (tokens[...].astype(F32) + branch).astype(BF)
    noised[...] = (
        levels[0] * generated.astype(F32) + levels[1] * fresh[...].astype(F32)
    ).astype(BF)
    columns[...] = weights[:, :, :HD]


def back_body(inv_root, place, *refs):
    blocks, refs = refs[:16], refs[16:]
    gram, noise_back, packed, weights, mine, normed, grad, whole = refs
    for k, b in enumerate(blocks):
        whole[pl.ds(pl.multiple_of(place[k] * HD, HD), HD), :] = b[:HD, :]
    back = jnp.concatenate([gram[g] for g in range(16)], axis=1)
    upstream = inv_root * (dot(back, whole[...], 1, 0) - noise_back[...])
    upstream = upstream.astype(BF)
    held = packed[...]
    query, keys, values = held[:HD], held[HD : 2 * HD], held[2 * HD :]
    chances = weights[...]
    grad_weights = dot(upstream.T, values, 1, 0)
    inner = jnp.sum(grad_weights * chances, axis=1, keepdims=True)
    grad_scores = (chances * (grad_weights - inner) * ROOT).astype(BF)
    grad_values = dot(upstream, chances.astype(BF), 1, 0)
    grad_query = dot(keys, grad_scores, 1, 1)
    grad_keys = dot(query, grad_scores, 1, 0)
    grad_packed = jnp.concatenate([grad_query, grad_keys, grad_values], axis=0).astype(BF)
    rows = dot(normed[...], grad_packed, 1, 1).astype(BF)
    for n in range(3):
        grad[:, n * F : (n + 1) * F, :] = rows[:, n * HD : (n + 1) * HD].reshape(16, F, HD)
    square = dot(whole[...], mine[:HD, :], 1, 1).astype(BF)
    grad[:, 3 * F :, :] = square.reshape(16, HD, HD)


def score_body(place, *refs):
    blocks, refs = refs[:16], refs[16:]
    weights, fake_chunk, fresh, gap, diff, whole = refs
    gather_slices(place, blocks, HD, whole)
    real_eps = project_slices(1, weights, whole)
    part = jnp.sum(jnp.abs(fresh[...].astype(F32) - real_eps))
    gap[...] = jnp.full((8, HD), part, F32)
    for k, b in enumerate(blocks):
        whole[pl.ds(pl.multiple_of(place[k] * HD, HD), HD), :] = b[:HD, :]
    chunk = jnp.concatenate([fake_chunk[g] for g in range(16)], axis=1)
    fake_eps = dot(chunk, whole[...], 1, 0)
    diff[...] = (real_eps - fake_eps).T


def out_body(inv_root, rows, square, noise, grad):
    total = jnp.zeros((F, HD), F32)
    for g in range(16):
        total = total + dot(rows[:, g * HD : (g + 1) * HD], square[g], 1, 0)
    grad[...] = inv_root * (total - noise[...])


def local(latent, noise, steps, gen_qkv, gen_out, real_qkv, real_out, fake_qkv, fake_out):
    fresh = noise[0]
    head = lax.axis_index("head")
    dp = lax.axis_index("dp")
    a, z = head // Z, head % Z
    offsets = (z + jnp.arange(Z)) % Z
    place = jnp.concatenate([a * Z + offsets, (1 - a) * Z + offsets]).astype(jnp.int32)
    levels = jnp.stack(noise_levels(steps[0]))
    inv_root = 1.0 / math.sqrt(L * 16)
    fresh_cols = lax.dynamic_slice_in_dim(fresh, head * F, F, 1).T

    start = dp // 2 * 16
    rows = jnp.where(
        dp % 2 == 0,
        lax.dynamic_slice_in_dim(gen_out, start, 16, 0),
        lax.dynamic_slice_in_dim(real_out, start, 16, 0),
    )
    rows = rows.reshape(16, 16, F).transpose(1, 0, 2)

    rows = lax.all_to_all(rows, "head", 0, 0)
    tokens = latent[0].T
    blocks = ring(jnp.concatenate([tokens, fake_out], axis=1))
    gen_mixed, fake_rows, gram = run(
        gen_body,
        [((HD, L), BF), ((F, INNER), BF), ((16, F, HD), BF)],
        [place],
        *blocks,
        gen_qkv,
        scratch=[pltpu.VMEM((D, L), BF)],
    )
    fake_full = lax.all_gather(fake_qkv, "dp", axis=0, tiled=True)
    gen_mixed, rows, fake_full = lax.optimization_barrier((gen_mixed, rows, fake_full))
    rows = rows.reshape(256, F).T
    weights = lax.all_gather(jnp.concatenate([fake_out, rows], axis=1), "dp", axis=0)

    gram = lax.psum_scatter(gram.reshape(D, HD), "dp", scatter_dimension=0, tiled=True)
    gram = lax.all_gather(jnp.pad(gram, ((0, 0), (0, 2 * HD))), "dp", axis=0)
    blocks = ring(gen_mixed)
    noised_part, fake_cols = run(
        noised_body,
        [((F, L), BF), ((16, F, HD), BF)],
        [place, levels],
        *blocks,
        weights,
        tokens,
        fresh_cols,
        scratch=[pltpu.VMEM((INNER, L), BF)],
    )

    blocks = ring(noised_part)
    (fake_cols,) = join(blocks, fake_cols)
    fake_chunk = lax.all_to_all(fake_cols, "head", 0, 0)
    mixed, packed, chances, normed = run(
        both_body,
        [((2 * HD, L), BF), ((3 * HD, L), BF), ((L, L), F32), ((D, L), BF)],
        [place],
        *blocks,
        fake_full,
        real_qkv,
    )
    blocks = ring(mixed)
    noise_back = dot(fake_cols.reshape(D, HD), fresh, 0, 1)
    noise_term = dot(fresh, mixed[:HD], 0, 1).astype(BF)
    fake_chunk, noise_back = join(blocks, fake_chunk, noise_back)
    noise_term = lax.psum_scatter(noise_term, "dp", scatter_dimension=0, tiled=True).astype(F32)
    (grad,) = run(
        functools.partial(back_body, inv_root),
        [((16, 3 * F + HD, HD), BF)],
        [place],
        *[(b, (slice(0, HD), slice(0, L))) for b in blocks],
        (gram, (slice(0, 16), slice(0, HD), slice(0, HD))),
        noise_back,
        packed,
        chances,
        (mixed, (slice(0, HD), slice(0, L))),
        normed,
        scratch=[pltpu.VMEM((INNER, L), BF)],
    )
    grad, weights = lax.optimization_barrier((grad, weights))
    got = lax.all_to_all(grad, "dp", 0, 0)
    gap, diff = run(
        score_body,
        [((8, HD), F32), ((L, F), F32)],
        [place],
        *blocks,
        weights,
        fake_chunk,
        fresh_cols,
        scratch=[pltpu.VMEM((INNER, L), BF)],
    )
    for d in (1, 2, 4):
        gap = gap + send(gap, "head", along(d))
    gap = gap + send(gap, "head", ACROSS)
    score_grad = (diff / (gap[0, 0] / (L * D) + 1e-05))[None]

    square = jnp.sum(got[:, 3 * F :].astype(F32), axis=0).astype(BF)
    fake_qkv_grad = jnp.concatenate(
        [jnp.sum(got[:, n * F : (n + 1) * F].astype(F32), axis=0) for n in range(3)], axis=1
    )
    (fake_out_grad,) = run(
        functools.partial(out_body, inv_root),
        [((F, HD), F32)],
        [],
        fake_rows,
        spread(square, "dp"),
        noise_term,
    )
    return (score_grad, fake_qkv_grad, fake_out_grad)


def solution(mesh):
    in_specs = (
        P("dp", None, "head"),
        P("dp", None, None),
        P("dp"),
        P(None, "head"),
        P("head", None),
        P(None, "head"),
        P("head", None),
        P("dp", "head"),
        P("dp", "head"),
    )
    out_specs = (P("dp", None, "head"), P("dp", "head"), P("dp", "head"))
    return jax.shard_map(local, mesh=mesh, in_specs=in_specs, out_specs=out_specs, check_vma=False)
```

```python
import functools
import math

import jax
import jax.numpy as jnp
from jax import lax
from jax.experimental import pallas as pl
from jax.experimental.pallas import tpu as pltpu
from jax.sharding import PartitionSpec as P

D = 3072
HD = 128
L = 512
F = 192
Z = 8
INNER = 2048
BF = jnp.bfloat16
F32 = jnp.float32
ROOT = 1.0 / math.sqrt(HD)

HEAD = [(a, z) for a in range(2) for z in range(Z)]
ACROSS = [(a * Z + z, (1 - a) * Z + z) for a, z in HEAD]


def along(d):
    return [(a * Z + z, a * Z + (z + d) % Z) for a, z in HEAD]


def send(v, axis, pairs):
    return lax.ppermute(v, axis, pairs)


def ring(block, wide=True):
    def up(v):
        return send(v, "head", along(1))

    def down(v):
        return send(v, "head", along(-1))

    def across(v):
        return send(v, "head", ACROSS)

    own = [block] + [None] * 7
    other = [None] * 8
    other[0] = across(block)
    own[1], own[7] = down(block), up(block)
    own[2], own[6] = down(own[1]), up(own[7])
    if wide:
        other[1], other[7] = across(own[1]), across(own[7])
    else:
        other[1], other[7] = down(other[0]), up(other[0])
    other[2], other[6] = down(other[1]), up(other[7])
    own[3], own[5] = down(own[2]), up(own[6])
    other[3], other[5] = down(other[2]), up(other[6])
    own[4] = down(own[3])
    other[4] = up(other[5])
    return own + other


def join(blocks, *arrays):
    both = lax.optimization_barrier((*blocks, *arrays))
    blocks[:] = both[:16]
    return both[16:]


def spread(block, axis):
    return lax.all_to_all(jnp.broadcast_to(block[None], (16,) + block.shape), axis, 0, 0)


def noise_levels(step):
    angle = (step.astype(F32) + 1.0) / 1001.0 * (math.pi / 2.0)
    return (jnp.cos(angle), jnp.sin(angle))


def dot(a, b, ca, cb):
    return lax.dot_general(a, b, (((ca,), (cb,)), ((), ())), preferred_element_type=F32)


class Late:
    def __init__(self, source, target, semaphore):
        self.copy = pltpu.make_async_copy(source, target, semaphore)
        self.target = target
        self.waited = False
        self.copy.start()

    def __getitem__(self, index):
        if not self.waited:
            self.copy.wait()
            self.waited = True
        return self.target[index]


def run(body, outs, scalars, *arrays, scratch=(), flops=10**9):
    cuts = [v[1] if isinstance(v, tuple) else None for v in arrays]
    arrays = [v[0] if isinstance(v, tuple) else v for v in arrays]
    shapes = [
        v.shape if c is None else tuple(s.stop - s.start for s in c)
        for v, c in zip(arrays, cuts)
    ]
    counts = [len(scalars), len(arrays), len(outs), len(arrays), len(scratch)]

    def kernel(*refs):
        groups, first = [], 0
        for count in counts:
            groups.append(refs[first : first + count])
            first += count
        numbers, sources, results, targets, spare = groups
        sources = [s if c is None else s.at[c] for s, c in zip(sources, cuts)]
        held = [Late(s, t, refs[-1].at[k]) for k, (s, t) in enumerate(zip(sources, targets))]
        body(*numbers, *held, *results, *spare)
        for late in held:
            if not late.waited:
                late.copy.wait()

    specs = [pl.BlockSpec(memory_space=pltpu.SMEM)] * len(scalars)
    specs += [pl.BlockSpec(memory_space=pl.ANY)] * len(arrays)
    return pl.pallas_call(
        kernel,
        out_shape=[jax.ShapeDtypeStruct(s, t) for s, t in outs],
        in_specs=specs,
        out_specs=[pl.BlockSpec(memory_space=pltpu.VMEM)] * len(outs),
        scratch_shapes=[
            *[pltpu.VMEM(s, v.dtype) for s, v in zip(shapes, arrays)],
            *scratch,
            pltpu.SemaphoreType.DMA((len(arrays),)),
        ],
        compiler_params=pltpu.CompilerParams(vmem_limit_bytes=56 * 1024 * 1024),
        cost_estimate=pl.CostEstimate(flops=flops, bytes_accessed=8 * 2**20, transcendentals=0),
    )(*scalars, *arrays)


def softmax_attend(packed):
    query = packed[:HD].T
    keys, values = packed[HD : 2 * HD], packed[2 * HD :]
    scores = dot(query, keys, 1, 0) * ROOT
    powers = jnp.exp(scores - jnp.max(scores, axis=1, keepdims=True))
    weights = powers / jnp.sum(powers, axis=1, keepdims=True)
    mixed = dot(values, weights.astype(BF), 1, 1).astype(BF)
    return weights, mixed


def normalize(place, blocks, normed):
    total = jnp.zeros((8, L), F32)
    for b in blocks:
        total = total + jnp.sum(b[:, :L].astype(F32).reshape(F // 8, 8, L), axis=0)
    mean = jnp.sum(total, axis=0, keepdims=True) / D
    total = jnp.zeros((8, L), F32)
    for b in blocks:
        center = b[:, :L].astype(F32) - mean
        total = total + jnp.sum((center * center).reshape(F // 8, 8, L), axis=0)
    scale = lax.rsqrt(jnp.sum(total, axis=0, keepdims=True) / D + 1e-06)
    for k, b in enumerate(blocks):
        rows = pl.ds(pl.multiple_of(place[k] * F, F), F)
        normed[rows, :] = ((b[:, :L].astype(F32) - mean) * scale).astype(BF)


def gather_slices(place, blocks, first, whole):
    for k, b in enumerate(blocks):
        for s in range(8):
            rows = pl.ds(pl.multiple_of(place[k] * 16 + s * 256, 16), 16)
            whole[rows, :] = b[first + s * 16 : first + s * 16 + 16, :]


def project_slices(which, weights, whole):
    total = jnp.zeros((F, L), F32)
    for s in range(8):
        weight = weights[2 * s + which, :, HD:]
        total = total + dot(weight, whole[s * 256 : (s + 1) * 256, :], 1, 0)
    return total


def gen_body(place, *refs):
    blocks, (weight, mixed, fake_rows, gram, normed) = refs[:16], refs[16:]
    normalize(place, blocks, normed)
    packed = dot(weight[...].T, normed[...], 1, 0).astype(BF)
    mixed[...] = softmax_attend(packed)[1]
    mine = blocks[0][:, L:].T
    for k, b in enumerate(blocks):
        part = b[:, L:]
        fake_rows[:, pl.ds(pl.multiple_of(place[k] * HD, HD), HD)] = part
        gram[place[k]] = dot(mine, part, 1, 0).astype(BF)


def both_body(place, *refs):
    blocks, refs = refs[:16], refs[16:]
    fake_weight, real_weight, fresh, mixed, packed, weights, normed, noise_term = refs
    normalize(place, blocks, normed)
    packed[...] = dot(fake_weight[...].T, normed[...], 1, 0).astype(BF)
    weights[...], fake_mixed = softmax_attend(packed[...])
    mixed[:HD, :] = fake_mixed
    noise_term[...] = dot(fake_mixed, fresh[...], 1, 0).T.astype(BF).reshape(16, F, HD)
    real_packed = dot(real_weight[...].T, normed[...], 1, 0).astype(BF)
    mixed[HD:, :] = softmax_attend(real_packed)[1]


def noised_body(place, levels, *refs):
    blocks, (weights, tokens, fresh, noised, columns, whole) = refs[:16], refs[16:]
    gather_slices(place, blocks, 0, whole)
    branch = project_slices(0, weights, whole)
    generated = (tokens[...].astype(F32) + branch).astype(BF)
    noised[...] = (
        levels[0] * generated.astype(F32) + levels[1] * fresh[...].astype(F32)
    ).astype(BF)
    columns[...] = weights[:, :, :HD]


def back_body(inv_root, place, *refs):
    blocks, refs = refs[:16], refs[16:]
    gram, noise_back, packed, weights, mine, noise_term, normed, grad, whole = refs
    for k, b in enumerate(blocks):
        whole[pl.ds(pl.multiple_of(place[k] * HD, HD), HD), :] = b[:HD, :]
    back = jnp.concatenate([gram[g] for g in range(16)], axis=1)
    upstream = inv_root * (dot(back, whole[...], 1, 0) - noise_back[...])
    upstream = upstream.astype(BF)
    held = packed[...]
    query, keys, values = held[:HD], held[HD : 2 * HD], held[2 * HD :]
    chances = weights[...]
    grad_weights = dot(upstream.T, values, 1, 0)
    inner = jnp.sum(grad_weights * chances, axis=1, keepdims=True)
    grad_scores = (chances * (grad_weights - inner) * ROOT).astype(BF)
    grad_values = dot(upstream, chances.astype(BF), 1, 0)
    grad_query = dot(keys, grad_scores, 1, 1)
    grad_keys = dot(query, grad_scores, 1, 0)
    grad_packed = jnp.concatenate([grad_query, grad_keys, grad_values], axis=0).astype(BF)
    rows = dot(normed[...], grad_packed, 1, 1).astype(BF)
    for n in range(3):
        grad[:, n * F : (n + 1) * F, :] = rows[:, n * HD : (n + 1) * HD].reshape(16, F, HD)
    square = dot(whole[...], mine[:HD, :], 1, 1).astype(BF)
    grad[:, 3 * F : 4 * F, :] = noise_term[...]
    grad[:, 4 * F :, :] = square.reshape(16, HD, HD)


def score_body(place, *refs):
    blocks, refs = refs[:16], refs[16:]
    weights, fake_chunk, fresh, gap, diff, whole = refs
    gather_slices(place, blocks, HD, whole)
    real_eps = project_slices(1, weights, whole)
    part = jnp.sum(jnp.abs(fresh[...].astype(F32) - real_eps))
    gap[...] = jnp.full((8, HD), part, F32)
    for k, b in enumerate(blocks):
        whole[pl.ds(pl.multiple_of(place[k] * HD, HD), HD), :] = b[:HD, :]
    chunk = jnp.concatenate([fake_chunk[g] for g in range(16)], axis=1)
    fake_eps = dot(chunk, whole[...], 1, 0)
    diff[...] = (real_eps - fake_eps).T


def out_body(inv_root, rows, square, noise, grad):
    total = jnp.zeros((F, HD), F32)
    for g in range(16):
        total = total + dot(rows[:, g * HD : (g + 1) * HD], square[g], 1, 0)
    grad[...] = inv_root * (total - noise[...])


def local(latent, noise, steps, gen_qkv, gen_out, real_qkv, real_out, fake_qkv, fake_out):
    fresh = noise[0]
    head = lax.axis_index("head")
    dp = lax.axis_index("dp")
    a, z = head // Z, head % Z
    offsets = (z + jnp.arange(Z)) % Z
    place = jnp.concatenate([a * Z + offsets, (1 - a) * Z + offsets]).astype(jnp.int32)
    levels = jnp.stack(noise_levels(steps[0]))
    inv_root = 1.0 / math.sqrt(L * 16)
    fresh_cols = lax.dynamic_slice_in_dim(fresh, head * F, F, 1).T

    start = dp // 2 * 16
    rows = jnp.where(
        dp % 2 == 0,
        lax.dynamic_slice_in_dim(gen_out, start, 16, 0),
        lax.dynamic_slice_in_dim(real_out, start, 16, 0),
    )
    rows = rows.reshape(16, 16, F).transpose(1, 0, 2)
    tokens = latent[0].T
    blocks = ring(jnp.concatenate([tokens, fake_out], axis=1))
    (rows,) = join(blocks, rows)
    rows = lax.all_to_all(rows, "head", 0, 0)
    gen_mixed, fake_rows, gram = run(
        gen_body,
        [((HD, L), BF), ((F, INNER), BF), ((16, HD, HD), BF)],
        [place],
        *blocks,
        gen_qkv,
        scratch=[pltpu.VMEM((D, L), BF)],
    )
    fake_full = lax.all_gather(fake_qkv, "dp", axis=0, tiled=True)
    gen_mixed, rows = lax.optimization_barrier((gen_mixed, rows))
    rows = rows.reshape(256, F).T
    weights = lax.all_gather(jnp.concatenate([fake_out, rows], axis=1), "dp", axis=0)

    gram = lax.all_to_all(gram, "dp", 0, 0)
    blocks = ring(gen_mixed, wide=False)
    noised_part, fake_cols = run(
        noised_body,
        [((F, L), BF), ((16, F, HD), BF)],
        [place, levels],
        *blocks,
        weights,
        tokens,
        fresh_cols,
        scratch=[pltpu.VMEM((INNER, L), BF)],
    )

    noised_part, gram = lax.optimization_barrier((noised_part, gram))
    gram = jnp.sum(gram.astype(F32), axis=0).astype(BF)
    gram = lax.all_gather(jnp.pad(gram, ((0, F - HD), (0, 2 * HD))), "dp", axis=0)
    blocks = ring(noised_part)
    (fake_cols,) = join(blocks, fake_cols)
    fake_chunk = lax.all_to_all(fake_cols, "head", 0, 0)
    noise_back = dot(fake_cols.reshape(D, HD), fresh, 0, 1)
    mixed, packed, chances, normed, noise_term = run(
        both_body,
        [
            ((2 * HD, L), BF),
            ((3 * HD, L), BF),
            ((L, L), F32),
            ((D, L), BF),
            ((16, F, HD), BF),
        ],
        [place],
        *blocks,
        fake_full,
        real_qkv,
        fresh,
    )
    blocks = ring(mixed)
    fake_chunk, noise_back = join(blocks, fake_chunk, noise_back)
    (grad,) = run(
        functools.partial(back_body, inv_root),
        [((16, 4 * F + HD, HD), BF)],
        [place],
        *[(b, (slice(0, HD), slice(0, L))) for b in blocks],
        (gram, (slice(0, 16), slice(0, HD), slice(0, HD))),
        noise_back,
        packed,
        chances,
        (mixed, (slice(0, HD), slice(0, L))),
        noise_term,
        normed,
        scratch=[pltpu.VMEM((INNER, L), BF)],
    )
    grad, weights = lax.optimization_barrier((grad, weights))
    got = lax.all_to_all(grad, "dp", 0, 0)
    gap, diff = run(
        score_body,
        [((8, HD), F32), ((L, F), F32)],
        [place],
        *blocks,
        weights,
        fake_chunk,
        fresh_cols,
        scratch=[pltpu.VMEM((INNER, L), BF)],
    )
    for d in (1, 2, 4):
        gap = gap + send(gap, "head", along(d))
    gap = gap + send(gap, "head", ACROSS)
    score_grad = (diff / (gap[0, 0] / (L * D) + 1e-05))[None]

    square = jnp.sum(got[:, 4 * F :].astype(F32), axis=0).astype(BF)
    fake_qkv_grad = jnp.concatenate(
        [jnp.sum(got[:, n * F : (n + 1) * F].astype(F32), axis=0) for n in range(3)], axis=1
    )
    (fake_out_grad,) = run(
        functools.partial(out_body, inv_root),
        [((F, HD), F32)],
        [],
        fake_rows,
        spread(square, "dp"),
        jnp.sum(got[:, 3 * F : 4 * F].astype(F32), axis=0),
    )
    return (score_grad, fake_qkv_grad, fake_out_grad)


def solution(mesh):
    in_specs = (
        P("dp", None, "head"),
        P("dp", None, None),
        P("dp"),
        P(None, "head"),
        P("head", None),
        P(None, "head"),
        P("head", None),
        P("dp", "head"),
        P("dp", "head"),
    )
    out_specs = (P("dp", None, "head"), P("dp", "head"), P("dp", "head"))
    return jax.shard_map(local, mesh=mesh, in_specs=in_specs, out_specs=out_specs, check_vma=False)
```

```python
import functools
import math

import jax
import jax.numpy as jnp
from jax import lax
from jax.experimental import pallas as pl
from jax.experimental.pallas import tpu as pltpu
from jax.sharding import PartitionSpec as P

D = 3072
HD = 128
L = 512
F = 192
Z = 8
INNER = 2048
BF = jnp.bfloat16
F32 = jnp.float32
ROOT = 1.0 / math.sqrt(HD)

HEAD = [(a, z) for a in range(2) for z in range(Z)]
ACROSS = [(a * Z + z, (1 - a) * Z + z) for a, z in HEAD]

CORE = [(i, i ^ 1) for i in range(16)]
CHIPS = [list(range(c, 16, 2)) for c in range(2)]


def along(d):
    return [(a * Z + z, a * Z + (z + d) % Z) for a, z in HEAD]


def send(v, axis, pairs):
    return lax.ppermute(v, axis, pairs)


def ring(block, wide=True):
    def up(v):
        return send(v, "head", along(1))

    def down(v):
        return send(v, "head", along(-1))

    def across(v):
        return send(v, "head", ACROSS)

    own = [block] + [None] * 7
    other = [None] * 8
    other[0] = across(block)
    own[1], own[7] = down(block), up(block)
    own[2], own[6] = down(own[1]), up(own[7])
    if wide:
        other[1], other[7] = across(own[1]), across(own[7])
    else:
        other[1], other[7] = down(other[0]), up(other[0])
    other[2], other[6] = down(other[1]), up(other[7])
    own[3], own[5] = down(own[2]), up(own[6])
    other[3], other[5] = down(other[2]), up(other[6])
    own[4] = down(own[3])
    other[4] = up(other[5])
    return own + other


def join(blocks, *arrays):
    both = lax.optimization_barrier((*blocks, *arrays))
    blocks[:] = both[:16]
    return both[16:]


def spread(block, axis):
    return lax.all_to_all(jnp.broadcast_to(block[None], (16,) + block.shape), axis, 0, 0)


def noise_levels(step):
    angle = (step.astype(F32) + 1.0) / 1001.0 * (math.pi / 2.0)
    return (jnp.cos(angle), jnp.sin(angle))


def dot(a, b, ca, cb):
    return lax.dot_general(a, b, (((ca,), (cb,)), ((), ())), preferred_element_type=F32)


class Late:
    def __init__(self, source, target, semaphore):
        self.copy = pltpu.make_async_copy(source, target, semaphore)
        self.target = target
        self.waited = False
        self.copy.start()

    def __getitem__(self, index):
        if not self.waited:
            self.copy.wait()
            self.waited = True
        return self.target[index]


def run(body, outs, scalars, *arrays, scratch=(), flops=10**9):
    cuts = [v[1] if isinstance(v, tuple) else None for v in arrays]
    arrays = [v[0] if isinstance(v, tuple) else v for v in arrays]
    shapes = [
        v.shape if c is None else tuple(s.stop - s.start for s in c)
        for v, c in zip(arrays, cuts)
    ]
    counts = [len(scalars), len(arrays), len(outs), len(arrays), len(scratch)]

    def kernel(*refs):
        groups, first = [], 0
        for count in counts:
            groups.append(refs[first : first + count])
            first += count
        numbers, sources, results, targets, spare = groups
        sources = [s if c is None else s.at[c] for s, c in zip(sources, cuts)]
        held = [Late(s, t, refs[-1].at[k]) for k, (s, t) in enumerate(zip(sources, targets))]
        body(*numbers, *held, *results, *spare)
        for late in held:
            if not late.waited:
                late.copy.wait()

    specs = [pl.BlockSpec(memory_space=pltpu.SMEM)] * len(scalars)
    specs += [pl.BlockSpec(memory_space=pl.ANY)] * len(arrays)
    return pl.pallas_call(
        kernel,
        out_shape=[jax.ShapeDtypeStruct(s, t) for s, t in outs],
        in_specs=specs,
        out_specs=[pl.BlockSpec(memory_space=pltpu.VMEM)] * len(outs),
        scratch_shapes=[
            *[pltpu.VMEM(s, v.dtype) for s, v in zip(shapes, arrays)],
            *scratch,
            pltpu.SemaphoreType.DMA((len(arrays),)),
        ],
        compiler_params=pltpu.CompilerParams(vmem_limit_bytes=56 * 1024 * 1024),
        cost_estimate=pl.CostEstimate(flops=flops, bytes_accessed=8 * 2**20, transcendentals=0),
    )(*scalars, *arrays)


def softmax_attend(packed):
    query = packed[:HD].T
    keys, values = packed[HD : 2 * HD], packed[2 * HD :]
    scores = dot(query, keys, 1, 0) * ROOT
    powers = jnp.exp(scores - jnp.max(scores, axis=1, keepdims=True))
    weights = powers / jnp.sum(powers, axis=1, keepdims=True)
    mixed = dot(values, weights.astype(BF), 1, 1).astype(BF)
    return weights, mixed


def normalize(place, blocks, normed):
    total = jnp.zeros((8, L), F32)
    for b in blocks:
        total = total + jnp.sum(b[:, :L].astype(F32).reshape(F // 8, 8, L), axis=0)
    mean = jnp.sum(total, axis=0, keepdims=True) / D
    total = jnp.zeros((8, L), F32)
    for b in blocks:
        center = b[:, :L].astype(F32) - mean
        total = total + jnp.sum((center * center).reshape(F // 8, 8, L), axis=0)
    scale = lax.rsqrt(jnp.sum(total, axis=0, keepdims=True) / D + 1e-06)
    for k, b in enumerate(blocks):
        rows = pl.ds(pl.multiple_of(place[k] * F, F), F)
        normed[rows, :] = ((b[:, :L].astype(F32) - mean) * scale).astype(BF)


def gather_slices(place, blocks, first, whole):
    for k, b in enumerate(blocks):
        for s in range(8):
            rows = pl.ds(pl.multiple_of(place[k] * 16 + s * 256, 16), 16)
            whole[rows, :] = b[first + s * 16 : first + s * 16 + 16, :]


def project_slices(which, weights, whole):
    total = jnp.zeros((F, L), F32)
    for s in range(8):
        weight = weights[2 * s + which, :, HD:]
        total = total + dot(weight, whole[s * 256 : (s + 1) * 256, :], 1, 0)
    return total


def gen_body(place, *refs):
    blocks, (weight, mixed, fake_rows, gram, normed) = refs[:16], refs[16:]
    normalize(place, blocks, normed)
    packed = dot(weight[...].T, normed[...], 1, 0).astype(BF)
    mixed[...] = softmax_attend(packed)[1]
    mine = blocks[0][:, L:].T
    for k, b in enumerate(blocks):
        part = b[:, L:]
        fake_rows[:, pl.ds(pl.multiple_of(place[k] * HD, HD), HD)] = part
        gram[place[k]] = dot(mine, part, 1, 0).astype(BF)


def both_body(place, *refs):
    blocks, refs = refs[:16], refs[16:]
    fake_weight, real_weight, fresh, mixed, packed, weights, normed, noise_term = refs
    normalize(place, blocks, normed)
    packed[...] = dot(fake_weight[...].T, normed[...], 1, 0).astype(BF)
    weights[...], fake_mixed = softmax_attend(packed[...])
    mixed[:HD, :] = fake_mixed
    noise_term[...] = dot(fake_mixed, fresh[...], 1, 0).T.astype(BF).reshape(16, F, HD)
    real_packed = dot(real_weight[...].T, normed[...], 1, 0).astype(BF)
    mixed[HD:, :] = softmax_attend(real_packed)[1]


def noised_body(place, levels, *refs):
    blocks, refs = refs[:16], refs[16:]
    weights, tokens, fresh, noised, columns, half, whole = refs
    gather_slices(place, blocks, 0, whole)
    branch = project_slices(0, weights, whole)
    generated = (tokens[...].astype(F32) + branch).astype(BF)
    noised[...] = (
        levels[0] * generated.astype(F32) + levels[1] * fresh[...].astype(F32)
    ).astype(BF)
    columns[...] = weights[:, :, :HD]
    half[...] = weights[:, pl.ds(pl.multiple_of(place[16] * (F // 2), 32), F // 2), :HD]


def back_body(inv_root, place, *refs):
    blocks, refs = refs[:16], refs[16:]
    gram, noise_back, packed, weights, mine, noise_term, normed, keep, give, whole, rows = refs
    for k, b in enumerate(blocks):
        whole[pl.ds(pl.multiple_of(place[k] * HD, HD), HD), :] = b[:HD, :]
    back = jnp.concatenate([gram[g] for g in range(16)], axis=1)
    upstream = inv_root * (dot(back, whole[...], 1, 0) - noise_back[...])
    upstream = upstream.astype(BF)
    held = packed[...]
    query, keys, values = held[:HD], held[HD : 2 * HD], held[2 * HD :]
    chances = weights[...]
    grad_weights = dot(upstream.T, values, 1, 0)
    inner = jnp.sum(grad_weights * chances, axis=1, keepdims=True)
    grad_scores = (chances * (grad_weights - inner) * ROOT).astype(BF)
    grad_values = dot(upstream, chances.astype(BF), 1, 0)
    grad_query = dot(keys, grad_scores, 1, 1)
    grad_keys = dot(query, grad_scores, 1, 0)
    grad_packed = jnp.concatenate([grad_query, grad_keys, grad_values], axis=0).astype(BF)
    rows[...] = dot(normed[...], grad_packed, 1, 1).astype(BF)
    square = dot(whole[...], mine[:HD, :], 1, 1).astype(BF)
    whole[:, :HD] = square
    for chip in range(8):
        for target, core in ((keep, place[16]), (give, 1 - place[16])):
            group = 2 * chip + core
            part = rows[pl.ds(pl.multiple_of(group * F, F), F), :]
            for n in range(3):
                target[chip, n * F : (n + 1) * F, :] = part[:, n * HD : (n + 1) * HD]
            target[chip, 3 * F : 4 * F, :] = noise_term[group]
            target[chip, 4 * F :, :] = whole[pl.ds(pl.multiple_of(group * HD, HD), HD), :HD]


def score_body(place, *refs):
    blocks, refs = refs[:16], refs[16:]
    weights, near, far, fresh, gap, diff, whole, chunk = refs
    gather_slices(place, blocks, HD, whole)
    real_eps = project_slices(1, weights, whole)
    part = jnp.sum(jnp.abs(fresh[...].astype(F32) - real_eps))
    gap[...] = jnp.full((8, HD), part, F32)
    for k, b in enumerate(blocks):
        whole[pl.ds(pl.multiple_of(place[k] * HD, HD), HD), :] = b[:HD, :]
    for part, core in ((near, place[16]), (far, 1 - place[16])):
        rows = pl.ds(pl.multiple_of(core * (F // 2), 32), F // 2)
        for g in range(16):
            chunk[rows, g * HD : (g + 1) * HD] = part[g]
    fake_eps = dot(chunk[...], whole[...], 1, 0)
    diff[...] = (real_eps - fake_eps).T


def out_body(inv_root, rows, square, noise, grad):
    total = jnp.zeros((F, HD), F32)
    for g in range(16):
        total = total + dot(rows[:, g * HD : (g + 1) * HD], square[g], 1, 0)
    grad[...] = inv_root * (total - noise[...])


def local(latent, noise, steps, gen_qkv, gen_out, real_qkv, real_out, fake_qkv, fake_out):
    fresh = noise[0]
    head = lax.axis_index("head")
    dp = lax.axis_index("dp")
    a, z = head // Z, head % Z
    offsets = (z + jnp.arange(Z)) % Z
    place = jnp.concatenate([a * Z + offsets, (1 - a) * Z + offsets, dp[None] % 2])
    place = place.astype(jnp.int32)
    levels = jnp.stack(noise_levels(steps[0]))
    inv_root = 1.0 / math.sqrt(L * 16)
    fresh_cols = lax.dynamic_slice_in_dim(fresh, head * F, F, 1).T

    start = dp // 2 * 16
    rows = jnp.where(
        dp % 2 == 0,
        lax.dynamic_slice_in_dim(gen_out, start, 16, 0),
        lax.dynamic_slice_in_dim(real_out, start, 16, 0),
    )
    rows = rows.reshape(16, 16, F).transpose(1, 0, 2)
    tokens = latent[0].T
    blocks = ring(jnp.concatenate([tokens, fake_out], axis=1))
    (rows,) = join(blocks, rows)
    rows = lax.all_to_all(rows, "head", 0, 0)
    gen_mixed, fake_rows, gram = run(
        gen_body,
        [((HD, L), BF), ((F, INNER), BF), ((16, HD, HD), BF)],
        [place],
        *blocks,
        gen_qkv,
        scratch=[pltpu.VMEM((D, L), BF)],
    )
    fake_full = lax.all_gather(fake_qkv, "dp", axis=0, tiled=True)
    gen_mixed, rows = lax.optimization_barrier((gen_mixed, rows))
    rows = rows.reshape(256, F).T
    weights = lax.all_gather(jnp.concatenate([fake_out, rows], axis=1), "dp", axis=0)

    gram = lax.all_to_all(gram, "dp", 0, 0)
    blocks = ring(gen_mixed, wide=False)
    noised_part, fake_cols, fake_half = run(
        noised_body,
        [((F, L), BF), ((16, F, HD), BF), ((16, F // 2, HD), BF)],
        [place, levels],
        *blocks,
        weights,
        tokens,
        fresh_cols,
        scratch=[pltpu.VMEM((INNER, L), BF)],
    )

    noised_part, gram = lax.optimization_barrier((noised_part, gram))
    gram = jnp.sum(gram.astype(F32), axis=0).astype(BF)
    gram = lax.all_gather(jnp.pad(gram, ((0, F - HD), (0, 2 * HD))), "dp", axis=0)
    blocks = ring(noised_part, wide=False)
    fake_cols, fake_half = join(blocks, fake_cols, fake_half)
    fake_near = lax.all_to_all(fake_half, "head", 0, 0)
    fake_far = send(fake_near, "dp", CORE)
    noise_back = dot(fake_cols.reshape(D, HD), fresh, 0, 1)
    mixed, packed, chances, normed, noise_term = run(
        both_body,
        [
            ((2 * HD, L), BF),
            ((3 * HD, L), BF),
            ((L, L), F32),
            ((D, L), BF),
            ((16, F, HD), BF),
        ],
        [place],
        *blocks,
        fake_full,
        real_qkv,
        fresh,
    )
    blocks = ring(mixed)
    fake_near, fake_far, noise_back = join(blocks, fake_near, fake_far, noise_back)
    keep, give = run(
        functools.partial(back_body, inv_root),
        [((8, 4 * F + HD, HD), BF), ((8, 4 * F + HD, HD), BF)],
        [place],
        *[(b, (slice(0, HD), slice(0, L))) for b in blocks],
        (gram, (slice(0, 16), slice(0, HD), slice(0, HD))),
        noise_back,
        packed,
        chances,
        (mixed, (slice(0, HD), slice(0, L))),
        noise_term,
        normed,
        scratch=[pltpu.VMEM((INNER, L), BF), pltpu.VMEM((D, 3 * HD), BF)],
    )
    give, weights = lax.optimization_barrier((give, weights))
    taken = send(give, "dp", CORE)
    gap, diff = run(
        score_body,
        [((8, HD), F32), ((L, F), F32)],
        [place],
        *blocks,
        weights,
        fake_near,
        fake_far,
        fresh_cols,
        scratch=[pltpu.VMEM((INNER, L), BF), pltpu.VMEM((F, INNER), BF)],
    )
    grad = (keep.astype(F32) + taken.astype(F32)).astype(BF)
    grad, gap = lax.optimization_barrier((grad, gap))
    got = lax.all_to_all(grad, "dp", 0, 0, axis_index_groups=CHIPS)
    for d in (1, 2, 4):
        gap = gap + send(gap, "head", along(d))
    gap = gap + send(gap, "head", ACROSS)
    score_grad = (diff / (gap[0, 0] / (L * D) + 1e-05))[None]

    square = jnp.sum(got[:, 4 * F :].astype(F32), axis=0).astype(BF)
    fake_qkv_grad = jnp.concatenate(
        [jnp.sum(got[:, n * F : (n + 1) * F].astype(F32), axis=0) for n in range(3)], axis=1
    )
    (fake_out_grad,) = run(
        functools.partial(out_body, inv_root),
        [((F, HD), F32)],
        [],
        fake_rows,
        spread(square, "dp"),
        jnp.sum(got[:, 3 * F : 4 * F].astype(F32), axis=0),
    )
    return (score_grad, fake_qkv_grad, fake_out_grad)


def solution(mesh):
    in_specs = (
        P("dp", None, "head"),
        P("dp", None, None),
        P("dp"),
        P(None, "head"),
        P("head", None),
        P(None, "head"),
        P("head", None),
        P("dp", "head"),
        P("dp", "head"),
    )
    out_specs = (P("dp", None, "head"), P("dp", "head"), P("dp", "head"))
    return jax.shard_map(local, mesh=mesh, in_specs=in_specs, out_specs=out_specs, check_vma=False)
```

```python
import functools
import math

import jax
import jax.numpy as jnp
from jax import lax
from jax.experimental import pallas as pl
from jax.experimental.pallas import tpu as pltpu
from jax.sharding import PartitionSpec as P

D = 3072
HD = 128
L = 512
F = 192
Z = 8
INNER = 2048
BF = jnp.bfloat16
F32 = jnp.float32
ROOT = 1.0 / math.sqrt(HD)

HEAD = [(a, z) for a in range(2) for z in range(Z)]
ACROSS = [(a * Z + z, (1 - a) * Z + z) for a, z in HEAD]

ACROSS_FAR = [(a * Z + z, (1 - a) * Z + (z + 4) % Z) for a, z in HEAD]
CORE = [(i, i ^ 1) for i in range(16)]
CHIPS = [list(range(c, 16, 2)) for c in range(2)]


def along(d):
    return [(a * Z + z, a * Z + (z + d) % Z) for a, z in HEAD]


def send(v, axis, pairs):
    return lax.ppermute(v, axis, pairs)


def ring(block, wide=1):
    def up(v):
        return send(v, "head", along(1))

    def down(v):
        return send(v, "head", along(-1))

    def across(v):
        return send(v, "head", ACROSS)

    own = [block] + [None] * 7
    other = [None] * 8
    other[0] = across(block)
    own[1], own[7] = down(block), up(block)
    own[2], own[6] = down(own[1]), up(own[7])
    if wide:
        other[1], other[7] = across(own[1]), across(own[7])
    else:
        other[1], other[7] = down(other[0]), up(other[0])
    if wide > 1:
        other[2], other[6] = across(own[2]), across(own[6])
    else:
        other[2], other[6] = down(other[1]), up(other[7])
    own[3], own[5] = down(own[2]), up(own[6])
    other[3], other[5] = down(other[2]), up(other[6])
    own[4] = down(own[3])
    other[4] = up(other[5])
    return own + other


def join(blocks, *arrays):
    both = lax.optimization_barrier((*blocks, *arrays))
    blocks[:] = both[:16]
    return both[16:]


def spread(block, axis):
    return lax.all_to_all(jnp.broadcast_to(block[None], (16,) + block.shape), axis, 0, 0)


def noise_levels(step):
    angle = (step.astype(F32) + 1.0) / 1001.0 * (math.pi / 2.0)
    return (jnp.cos(angle), jnp.sin(angle))


def dot(a, b, ca, cb):
    return lax.dot_general(a, b, (((ca,), (cb,)), ((), ())), preferred_element_type=F32)


class Late:
    def __init__(self, source, target, semaphore):
        self.copy = pltpu.make_async_copy(source, target, semaphore)
        self.target = target
        self.waited = False
        self.copy.start()

    def __getitem__(self, index):
        if not self.waited:
            self.copy.wait()
            self.waited = True
        return self.target[index]


def run(body, outs, scalars, *arrays, scratch=(), flops=10**9):
    cuts = [v[1] if isinstance(v, tuple) else None for v in arrays]
    arrays = [v[0] if isinstance(v, tuple) else v for v in arrays]
    shapes = [
        v.shape if c is None else tuple(s.stop - s.start for s in c)
        for v, c in zip(arrays, cuts)
    ]
    counts = [len(scalars), len(arrays), len(outs), len(arrays), len(scratch)]

    def kernel(*refs):
        groups, first = [], 0
        for count in counts:
            groups.append(refs[first : first + count])
            first += count
        numbers, sources, results, targets, spare = groups
        sources = [s if c is None else s.at[c] for s, c in zip(sources, cuts)]
        held = [Late(s, t, refs[-1].at[k]) for k, (s, t) in enumerate(zip(sources, targets))]
        body(*numbers, *held, *results, *spare)
        for late in held:
            if not late.waited:
                late.copy.wait()

    specs = [pl.BlockSpec(memory_space=pltpu.SMEM)] * len(scalars)
    specs += [pl.BlockSpec(memory_space=pl.ANY)] * len(arrays)
    return pl.pallas_call(
        kernel,
        out_shape=[jax.ShapeDtypeStruct(s, t) for s, t in outs],
        in_specs=specs,
        out_specs=[pl.BlockSpec(memory_space=pltpu.VMEM)] * len(outs),
        scratch_shapes=[
            *[pltpu.VMEM(s, v.dtype) for s, v in zip(shapes, arrays)],
            *scratch,
            pltpu.SemaphoreType.DMA((len(arrays),)),
        ],
        compiler_params=pltpu.CompilerParams(vmem_limit_bytes=56 * 1024 * 1024),
        cost_estimate=pl.CostEstimate(flops=flops, bytes_accessed=8 * 2**20, transcendentals=0),
    )(*scalars, *arrays)


def softmax_attend(packed):
    query = packed[:HD].T
    keys, values = packed[HD : 2 * HD], packed[2 * HD :]
    scores = dot(query, keys, 1, 0) * ROOT
    powers = jnp.exp(scores - jnp.max(scores, axis=1, keepdims=True))
    weights = powers / jnp.sum(powers, axis=1, keepdims=True)
    mixed = dot(values, weights.astype(BF), 1, 1).astype(BF)
    return weights, mixed


def normalize(place, blocks, normed):
    total = jnp.zeros((8, L), F32)
    for b in blocks:
        total = total + jnp.sum(b[:, :L].astype(F32).reshape(F // 8, 8, L), axis=0)
    mean = jnp.sum(total, axis=0, keepdims=True) / D
    total = jnp.zeros((8, L), F32)
    for b in blocks:
        center = b[:, :L].astype(F32) - mean
        total = total + jnp.sum((center * center).reshape(F // 8, 8, L), axis=0)
    scale = lax.rsqrt(jnp.sum(total, axis=0, keepdims=True) / D + 1e-06)
    for k, b in enumerate(blocks):
        rows = pl.ds(pl.multiple_of(place[k] * F, F), F)
        normed[rows, :] = ((b[:, :L].astype(F32) - mean) * scale).astype(BF)


def gather_slices(place, blocks, first, whole):
    for k, b in enumerate(blocks):
        for s in range(8):
            rows = pl.ds(pl.multiple_of(place[k] * 16 + s * 256, 16), 16)
            whole[rows, :] = b[first + s * 16 : first + s * 16 + 16, :]


def project_slices(which, weights, whole):
    total = jnp.zeros((F, L), F32)
    for s in range(8):
        weight = weights[2 * s + which, :, HD:]
        total = total + dot(weight, whole[s * 256 : (s + 1) * 256, :], 1, 0)
    return total


def gen_body(place, *refs):
    blocks, (weight, mixed, fake_rows, gram, normed) = refs[:16], refs[16:]
    normalize(place, blocks, normed)
    packed = dot(weight[...].T, normed[...], 1, 0).astype(BF)
    mixed[...] = softmax_attend(packed)[1]
    mine = blocks[0][:, L:].T
    for k, b in enumerate(blocks):
        part = b[:, L:]
        fake_rows[:, pl.ds(pl.multiple_of(place[k] * HD, HD), HD)] = part
        gram[place[k]] = dot(mine, part, 1, 0).astype(BF)


def both_body(place, *refs):
    blocks, refs = refs[:16], refs[16:]
    fake_weight, real_weight, fresh, columns, refs = *refs[:4], refs[4:]
    mixed, packed, weights, normed, noise_term, noise_back = refs
    normalize(place, blocks, normed)
    packed[...] = dot(fake_weight[...].T, normed[...], 1, 0).astype(BF)
    weights[...], fake_mixed = softmax_attend(packed[...])
    mixed[:HD, :] = fake_mixed
    noise_term[...] = dot(fake_mixed, fresh[...], 1, 0).T.astype(BF).reshape(16, F, HD)
    back = columns[...].reshape(D, HD).T
    noise_back[...] = dot(back, fresh[...], 1, 1)
    real_packed = dot(real_weight[...].T, normed[...], 1, 0).astype(BF)
    mixed[HD:, :] = softmax_attend(real_packed)[1]


def noised_body(place, levels, *refs):
    blocks, refs = refs[:16], refs[16:]
    weights, tokens, fresh, noised, columns, half, whole = refs
    gather_slices(place, blocks, 0, whole)
    branch = project_slices(0, weights, whole)
    generated = (tokens[...].astype(F32) + branch).astype(BF)
    noised[...] = (
        levels[0] * generated.astype(F32) + levels[1] * fresh[...].astype(F32)
    ).astype(BF)
    columns[...] = weights[:, :, :HD]
    half[...] = weights[:, pl.ds(pl.multiple_of(place[16] * (F // 2), 32), F // 2), :HD]


def back_body(inv_root, place, *refs):
    blocks, refs = refs[:16], refs[16:]
    gram, noise_back, packed, weights, mine, noise_term, normed, keep, give, whole, rows = refs
    for k, b in enumerate(blocks):
        whole[pl.ds(pl.multiple_of(place[k] * HD, HD), HD), :] = b[:HD, :]
    back = jnp.concatenate([gram[g] for g in range(16)], axis=1)
    upstream = inv_root * (dot(back, whole[...], 1, 0) - noise_back[...])
    upstream = upstream.astype(BF)
    held = packed[...]
    query, keys, values = held[:HD], held[HD : 2 * HD], held[2 * HD :]
    chances = weights[...]
    grad_weights = dot(upstream.T, values, 1, 0)
    inner = jnp.sum(grad_weights * chances, axis=1, keepdims=True)
    grad_scores = (chances * (grad_weights - inner) * ROOT).astype(BF)
    grad_values = dot(upstream, chances.astype(BF), 1, 0)
    grad_query = dot(keys, grad_scores, 1, 1)
    grad_keys = dot(query, grad_scores, 1, 0)
    grad_packed = jnp.concatenate([grad_query, grad_keys, grad_values], axis=0).astype(BF)
    rows[...] = dot(normed[...], grad_packed, 1, 1).astype(BF)
    square = dot(whole[...], mine[:HD, :], 1, 1).astype(BF)
    whole[:, :HD] = square
    for chip in range(8):
        for target, core in ((keep, place[16]), (give, 1 - place[16])):
            group = 2 * chip + core
            part = rows[pl.ds(pl.multiple_of(group * F, F), F), :]
            for n in range(3):
                target[chip, n * F : (n + 1) * F, :] = part[:, n * HD : (n + 1) * HD]
            target[chip, 3 * F : 4 * F, :] = noise_term[group]
            target[chip, 4 * F :, :] = whole[pl.ds(pl.multiple_of(group * HD, HD), HD), :HD]


def score_body(place, *refs):
    blocks, refs = refs[:16], refs[16:]
    weights, near, far, fresh, gap, diff, whole, chunk = refs
    gather_slices(place, blocks, HD, whole)
    real_eps = project_slices(1, weights, whole)
    part = jnp.sum(jnp.abs(fresh[...].astype(F32) - real_eps))
    gap[...] = jnp.full((8, HD), part, F32)
    for k, b in enumerate(blocks):
        whole[pl.ds(pl.multiple_of(place[k] * HD, HD), HD), :] = b[:HD, :]
    for part, core in ((near, place[16]), (far, 1 - place[16])):
        rows = pl.ds(pl.multiple_of(core * (F // 2), 32), F // 2)
        for g in range(16):
            chunk[rows, g * HD : (g + 1) * HD] = part[g]
    fake_eps = dot(chunk[...], whole[...], 1, 0)
    diff[...] = (real_eps - fake_eps).T


def out_body(inv_root, rows, square, noise, grad):
    total = jnp.zeros((F, HD), F32)
    for g in range(16):
        total = total + dot(rows[:, g * HD : (g + 1) * HD], square[g], 1, 0)
    grad[...] = inv_root * (total - noise[...])


def local(latent, noise, steps, gen_qkv, gen_out, real_qkv, real_out, fake_qkv, fake_out):
    fresh = noise[0]
    head = lax.axis_index("head")
    dp = lax.axis_index("dp")
    a, z = head // Z, head % Z
    offsets = (z + jnp.arange(Z)) % Z
    place = jnp.concatenate([a * Z + offsets, (1 - a) * Z + offsets, dp[None] % 2])
    place = place.astype(jnp.int32)
    levels = jnp.stack(noise_levels(steps[0]))
    inv_root = 1.0 / math.sqrt(L * 16)
    fresh_cols = lax.dynamic_slice_in_dim(fresh, head * F, F, 1).T

    start = dp // 2 * 16
    rows = jnp.where(
        dp % 2 == 0,
        lax.dynamic_slice_in_dim(gen_out, start, 16, 0),
        lax.dynamic_slice_in_dim(real_out, start, 16, 0),
    )
    rows = rows.reshape(16, 16, F).transpose(1, 0, 2)
    tokens = latent[0].T
    blocks = ring(jnp.concatenate([tokens, fake_out], axis=1), wide=2)
    (rows,) = join(blocks, rows)
    rows = lax.all_to_all(rows, "head", 0, 0)
    gen_mixed, fake_rows, gram = run(
        gen_body,
        [((HD, L), BF), ((F, INNER), BF), ((16, HD, HD), BF)],
        [place],
        *blocks,
        gen_qkv,
        scratch=[pltpu.VMEM((D, L), BF)],
    )
    fake_full = lax.all_gather(fake_qkv, "dp", axis=0, tiled=True)
    gen_mixed, rows = lax.optimization_barrier((gen_mixed, rows))
    rows = rows.reshape(256, F).T
    weights = lax.all_gather(jnp.concatenate([fake_out, rows], axis=1), "dp", axis=0)

    gram = lax.all_to_all(gram, "dp", 0, 0)
    blocks = ring(gen_mixed, wide=0)
    noised_part, fake_cols, fake_half = run(
        noised_body,
        [((F, L), BF), ((16, F, HD), BF), ((16, F // 2, HD), BF)],
        [place, levels],
        *blocks,
        weights,
        tokens,
        fresh_cols,
        scratch=[pltpu.VMEM((INNER, L), BF)],
    )

    noised_part, gram = lax.optimization_barrier((noised_part, gram))
    gram = jnp.sum(gram.astype(F32), axis=0).astype(BF)
    gram = lax.all_gather(jnp.pad(gram, ((0, F - HD), (0, 2 * HD))), "dp", axis=0)
    blocks = ring(noised_part, wide=0)
    fake_cols, fake_half = join(blocks, fake_cols, fake_half)
    fake_near = lax.all_to_all(fake_half, "head", 0, 0)
    mixed, packed, chances, normed, noise_term, noise_back = run(
        both_body,
        [
            ((2 * HD, L), BF),
            ((3 * HD, L), BF),
            ((L, L), F32),
            ((D, L), BF),
            ((16, F, HD), BF),
            ((HD, L), F32),
        ],
        [place],
        *blocks,
        fake_full,
        real_qkv,
        fresh,
        fake_cols,
    )
    mixed, fake_near = lax.optimization_barrier((mixed, fake_near))
    fake_far = send(fake_near, "dp", CORE)
    blocks = ring(mixed)
    fake_near, fake_far = join(blocks, fake_near, fake_far)
    keep, give = run(
        functools.partial(back_body, inv_root),
        [((8, 4 * F + HD, HD), BF), ((8, 4 * F + HD, HD), BF)],
        [place],
        *[(b, (slice(0, HD), slice(0, L))) for b in blocks],
        (gram, (slice(0, 16), slice(0, HD), slice(0, HD))),
        noise_back,
        packed,
        chances,
        (mixed, (slice(0, HD), slice(0, L))),
        noise_term,
        normed,
        scratch=[pltpu.VMEM((INNER, L), BF), pltpu.VMEM((D, 3 * HD), BF)],
    )
    give, weights = lax.optimization_barrier((give, weights))
    taken = send(give, "dp", CORE)
    gap, diff = run(
        score_body,
        [((8, HD), F32), ((L, F), F32)],
        [place],
        *blocks,
        weights,
        fake_near,
        fake_far,
        fresh_cols,
        scratch=[pltpu.VMEM((INNER, L), BF), pltpu.VMEM((F, INNER), BF)],
    )
    grad = (keep.astype(F32) + taken.astype(F32)).astype(BF)
    grad, gap = lax.optimization_barrier((grad, gap))
    got = lax.all_to_all(grad, "dp", 0, 0, axis_index_groups=CHIPS)
    gap = gap + sum(send(gap, "head", along(d)) for d in (1, 2, 3))
    gap = gap + sum(send(gap, "head", p) for p in (along(4), ACROSS, ACROSS_FAR))
    score_grad = (diff / (gap[0, 0] / (L * D) + 1e-05))[None]

    square = jnp.sum(got[:, 4 * F :].astype(F32), axis=0).astype(BF)
    fake_qkv_grad = jnp.concatenate(
        [jnp.sum(got[:, n * F : (n + 1) * F].astype(F32), axis=0) for n in range(3)], axis=1
    )
    (fake_out_grad,) = run(
        functools.partial(out_body, inv_root),
        [((F, HD), F32)],
        [],
        fake_rows,
        spread(square, "dp"),
        jnp.sum(got[:, 3 * F : 4 * F].astype(F32), axis=0),
    )
    return (score_grad, fake_qkv_grad, fake_out_grad)


def solution(mesh):
    in_specs = (
        P("dp", None, "head"),
        P("dp", None, None),
        P("dp"),
        P(None, "head"),
        P("head", None),
        P(None, "head"),
        P("head", None),
        P("dp", "head"),
        P("dp", "head"),
    )
    out_specs = (P("dp", None, "head"), P("dp", "head"), P("dp", "head"))
    return jax.shard_map(local, mesh=mesh, in_specs=in_specs, out_specs=out_specs, check_vma=False)
```

```python
import functools
import math

import jax
import jax.numpy as jnp
from jax import lax
from jax.experimental import pallas as pl
from jax.experimental.pallas import tpu as pltpu
from jax.sharding import PartitionSpec as P

D = 3072
HD = 128
L = 512
F = 192
Z = 8
INNER = 2048
BF = jnp.bfloat16
F32 = jnp.float32
ROOT = 1.0 / math.sqrt(HD)

HEAD = [(a, z) for a in range(2) for z in range(Z)]
ACROSS = [(a * Z + z, (1 - a) * Z + z) for a, z in HEAD]

CORE = [(i, i ^ 1) for i in range(16)]
CHIPS = [list(range(c, 16, 2)) for c in range(2)]


def along(d):
    return [(a * Z + z, a * Z + (z + d) % Z) for a, z in HEAD]


def send(v, axis, pairs):
    return lax.ppermute(v, axis, pairs)


def ring(block, wide=True):
    def up(v):
        return send(v, "head", along(1))

    def down(v):
        return send(v, "head", along(-1))

    def across(v):
        return send(v, "head", ACROSS)

    own = [block] + [None] * 7
    other = [None] * 8
    other[0] = across(block)
    own[1], own[7] = down(block), up(block)
    own[2], own[6] = down(own[1]), up(own[7])
    if wide:
        other[1], other[7] = across(own[1]), across(own[7])
    else:
        other[1], other[7] = down(other[0]), up(other[0])
    other[2], other[6] = down(other[1]), up(other[7])
    own[3], own[5] = down(own[2]), up(own[6])
    own[4] = down(own[3])
    other[4] = send(other[6], "head", along(2))
    other[3], other[5] = down(other[2]), up(other[6])
    return own + other


def join(blocks, *arrays):
    both = lax.optimization_barrier((*blocks, *arrays))
    blocks[:] = both[:16]
    return both[16:]


def spread(block, axis):
    return lax.all_to_all(jnp.broadcast_to(block[None], (16,) + block.shape), axis, 0, 0)


def noise_levels(step):
    angle = (step.astype(F32) + 1.0) / 1001.0 * (math.pi / 2.0)
    return (jnp.cos(angle), jnp.sin(angle))


def dot(a, b, ca, cb):
    return lax.dot_general(a, b, (((ca,), (cb,)), ((), ())), preferred_element_type=F32)


class Late:
    def __init__(self, source, target, semaphore):
        self.copy = pltpu.make_async_copy(source, target, semaphore)
        self.target = target
        self.waited = False
        self.copy.start()

    def __getitem__(self, index):
        if not self.waited:
            self.copy.wait()
            self.waited = True
        return self.target[index]


def run(body, outs, scalars, *arrays, scratch=(), flops=10**9):
    cuts = [v[1] if isinstance(v, tuple) else None for v in arrays]
    arrays = [v[0] if isinstance(v, tuple) else v for v in arrays]
    shapes = [
        v.shape if c is None else tuple(s.stop - s.start for s in c)
        for v, c in zip(arrays, cuts)
    ]
    counts = [len(scalars), len(arrays), len(outs), len(arrays), len(scratch)]

    def kernel(*refs):
        groups, first = [], 0
        for count in counts:
            groups.append(refs[first : first + count])
            first += count
        numbers, sources, results, targets, spare = groups
        sources = [s if c is None else s.at[c] for s, c in zip(sources, cuts)]
        held = [Late(s, t, refs[-1].at[k]) for k, (s, t) in enumerate(zip(sources, targets))]
        body(*numbers, *held, *results, *spare)
        for late in held:
            if not late.waited:
                late.copy.wait()

    specs = [pl.BlockSpec(memory_space=pltpu.SMEM)] * len(scalars)
    specs += [pl.BlockSpec(memory_space=pl.ANY)] * len(arrays)
    return pl.pallas_call(
        kernel,
        out_shape=[jax.ShapeDtypeStruct(s, t) for s, t in outs],
        in_specs=specs,
        out_specs=[pl.BlockSpec(memory_space=pltpu.VMEM)] * len(outs),
        scratch_shapes=[
            *[pltpu.VMEM(s, v.dtype) for s, v in zip(shapes, arrays)],
            *scratch,
            pltpu.SemaphoreType.DMA((len(arrays),)),
        ],
        compiler_params=pltpu.CompilerParams(vmem_limit_bytes=56 * 1024 * 1024),
        cost_estimate=pl.CostEstimate(flops=flops, bytes_accessed=8 * 2**20, transcendentals=0),
    )(*scalars, *arrays)


def softmax_attend(packed):
    query = packed[:HD].T
    keys, values = packed[HD : 2 * HD], packed[2 * HD :]
    scores = dot(query, keys, 1, 0) * ROOT
    powers = jnp.exp(scores - jnp.max(scores, axis=1, keepdims=True))
    weights = powers / jnp.sum(powers, axis=1, keepdims=True)
    mixed = dot(values, weights.astype(BF), 1, 1).astype(BF)
    return weights, mixed


def normalize(place, blocks, normed):
    total = jnp.zeros((8, L), F32)
    for b in blocks:
        total = total + jnp.sum(b[:, :L].astype(F32).reshape(F // 8, 8, L), axis=0)
    mean = jnp.sum(total, axis=0, keepdims=True) / D
    total = jnp.zeros((8, L), F32)
    for b in blocks:
        center = b[:, :L].astype(F32) - mean
        total = total + jnp.sum((center * center).reshape(F // 8, 8, L), axis=0)
    scale = lax.rsqrt(jnp.sum(total, axis=0, keepdims=True) / D + 1e-06)
    for k, b in enumerate(blocks):
        rows = pl.ds(pl.multiple_of(place[k] * F, F), F)
        normed[rows, :] = ((b[:, :L].astype(F32) - mean) * scale).astype(BF)


def gather_slices(place, blocks, first, whole):
    for k, b in enumerate(blocks):
        for s in range(8):
            rows = pl.ds(pl.multiple_of(place[k] * 16 + s * 256, 16), 16)
            whole[rows, :] = b[first + s * 16 : first + s * 16 + 16, :]


def project_slices(which, weights, whole):
    total = jnp.zeros((F, L), F32)
    for s in range(8):
        weight = weights[2 * s + which, :, HD:]
        total = total + dot(weight, whole[s * 256 : (s + 1) * 256, :], 1, 0)
    return total


def gen_body(place, *refs):
    blocks, (weight, mixed, fake_rows, gram, normed) = refs[:16], refs[16:]
    normalize(place, blocks, normed)
    packed = dot(weight[...].T, normed[...], 1, 0).astype(BF)
    mixed[...] = softmax_attend(packed)[1]
    mine = blocks[0][:, L:].T
    for k, b in enumerate(blocks):
        part = b[:, L:]
        fake_rows[:, pl.ds(pl.multiple_of(place[k] * HD, HD), HD)] = part
        gram[place[k]] = dot(mine, part, 1, 0).astype(BF)


def both_body(place, *refs):
    blocks, refs = refs[:16], refs[16:]
    fake_weight, real_weight, fresh, columns, refs = *refs[:4], refs[4:]
    mixed, packed, weights, normed, noise_term, noise_back = refs
    normalize(place, blocks, normed)
    packed[...] = dot(fake_weight[...].T, normed[...], 1, 0).astype(BF)
    weights[...], fake_mixed = softmax_attend(packed[...])
    mixed[:HD, :] = fake_mixed
    noise_term[...] = dot(fake_mixed, fresh[...], 1, 0).T.astype(BF).reshape(16, F, HD)
    back = columns[...].reshape(D, HD).T
    noise_back[...] = dot(back, fresh[...], 1, 1)
    real_packed = dot(real_weight[...].T, normed[...], 1, 0).astype(BF)
    mixed[HD:, :] = softmax_attend(real_packed)[1]


def noised_body(place, levels, *refs):
    blocks, refs = refs[:16], refs[16:]
    weights, tokens, fresh, noised, columns, half, whole = refs
    gather_slices(place, blocks, 0, whole)
    branch = project_slices(0, weights, whole)
    generated = (tokens[...].astype(F32) + branch).astype(BF)
    noised[...] = (
        levels[0] * generated.astype(F32) + levels[1] * fresh[...].astype(F32)
    ).astype(BF)
    columns[...] = weights[:, :, :HD]
    half[...] = weights[:, pl.ds(pl.multiple_of(place[16] * (F // 2), 32), F // 2), :HD]


def back_body(inv_root, place, *refs):
    blocks, refs = refs[:16], refs[16:]
    gram, noise_back, packed, weights, mine, noise_term, normed, keep, give, whole, rows = refs
    for k, b in enumerate(blocks):
        whole[pl.ds(pl.multiple_of(place[k] * HD, HD), HD), :] = b[:HD, :]
    back = jnp.concatenate([gram[g] for g in range(16)], axis=1)
    upstream = inv_root * (dot(back, whole[...], 1, 0) - noise_back[...])
    upstream = upstream.astype(BF)
    held = packed[...]
    query, keys, values = held[:HD], held[HD : 2 * HD], held[2 * HD :]
    chances = weights[...]
    grad_weights = dot(upstream.T, values, 1, 0)
    inner = jnp.sum(grad_weights * chances, axis=1, keepdims=True)
    grad_scores = (chances * (grad_weights - inner) * ROOT).astype(BF)
    grad_values = dot(upstream, chances.astype(BF), 1, 0)
    grad_query = dot(keys, grad_scores, 1, 1)
    grad_keys = dot(query, grad_scores, 1, 0)
    grad_packed = jnp.concatenate([grad_query, grad_keys, grad_values], axis=0).astype(BF)
    rows[...] = dot(normed[...], grad_packed, 1, 1).astype(BF)
    square = dot(whole[...], mine[:HD, :], 1, 1).astype(BF)
    whole[:, :HD] = square
    for chip in range(8):
        for target, core in ((keep, place[16]), (give, 1 - place[16])):
            group = 2 * chip + core
            part = rows[pl.ds(pl.multiple_of(group * F, F), F), :]
            for n in range(3):
                target[chip, n * F : (n + 1) * F, :] = part[:, n * HD : (n + 1) * HD]
            target[chip, 3 * F : 4 * F, :] = noise_term[group]
            target[chip, 4 * F :, :] = whole[pl.ds(pl.multiple_of(group * HD, HD), HD), :HD]


def score_body(place, *refs):
    blocks, refs = refs[:16], refs[16:]
    weights, near, far, fresh, gap, diff, whole, chunk = refs
    gather_slices(place, blocks, HD, whole)
    real_eps = project_slices(1, weights, whole)
    part = jnp.sum(jnp.abs(fresh[...].astype(F32) - real_eps))
    gap[...] = jnp.full((8, HD), part, F32)
    for k, b in enumerate(blocks):
        whole[pl.ds(pl.multiple_of(place[k] * HD, HD), HD), :] = b[:HD, :]
    for part, core in ((near, place[16]), (far, 1 - place[16])):
        rows = pl.ds(pl.multiple_of(core * (F // 2), 32), F // 2)
        for g in range(16):
            chunk[rows, g * HD : (g + 1) * HD] = part[g]
    fake_eps = dot(chunk[...], whole[...], 1, 0)
    diff[...] = (real_eps - fake_eps).T


def out_body(inv_root, rows, square, noise, grad):
    total = jnp.zeros((F, HD), F32)
    for g in range(16):
        total = total + dot(rows[:, g * HD : (g + 1) * HD], square[g], 1, 0)
    grad[...] = inv_root * (total - noise[...])


def local(latent, noise, steps, gen_qkv, gen_out, real_qkv, real_out, fake_qkv, fake_out):
    fresh = noise[0]
    head = lax.axis_index("head")
    dp = lax.axis_index("dp")
    a, z = head // Z, head % Z
    offsets = (z + jnp.arange(Z)) % Z
    place = jnp.concatenate([a * Z + offsets, (1 - a) * Z + offsets, dp[None] % 2])
    place = place.astype(jnp.int32)
    levels = jnp.stack(noise_levels(steps[0]))
    inv_root = 1.0 / math.sqrt(L * 16)
    fresh_cols = lax.dynamic_slice_in_dim(fresh, head * F, F, 1).T

    start = dp // 2 * 16
    rows = jnp.where(
        dp % 2 == 0,
        lax.dynamic_slice_in_dim(gen_out, start, 16, 0),
        lax.dynamic_slice_in_dim(real_out, start, 16, 0),
    )
    rows = rows.reshape(16, 16, F).transpose(1, 0, 2)
    tokens = latent[0].T
    blocks = ring(jnp.concatenate([tokens, fake_out], axis=1))
    (rows,) = join(blocks, rows)
    rows = lax.all_to_all(rows, "head", 0, 0)
    gen_mixed, fake_rows, gram = run(
        gen_body,
        [((HD, L), BF), ((F, INNER), BF), ((16, HD, HD), BF)],
        [place],
        *blocks,
        gen_qkv,
        scratch=[pltpu.VMEM((D, L), BF)],
    )
    fake_full = lax.all_gather(fake_qkv, "dp", axis=0, tiled=True)
    gen_mixed, rows = lax.optimization_barrier((gen_mixed, rows))
    rows = rows.reshape(256, F).T
    weights = lax.all_gather(jnp.concatenate([fake_out, rows], axis=1), "dp", axis=0)

    gram = lax.all_to_all(gram, "dp", 0, 0)
    blocks = ring(gen_mixed, wide=False)
    noised_part, fake_cols, fake_half = run(
        noised_body,
        [((F, L), BF), ((16, F, HD), BF), ((16, F // 2, HD), BF)],
        [place, levels],
        *blocks,
        weights,
        tokens,
        fresh_cols,
        scratch=[pltpu.VMEM((INNER, L), BF)],
    )

    noised_part, gram = lax.optimization_barrier((noised_part, gram))
    gram = jnp.sum(gram.astype(F32), axis=0).astype(BF)
    gram = lax.all_gather(jnp.pad(gram, ((0, F - HD), (0, 2 * HD))), "dp", axis=0)
    blocks = ring(noised_part, wide=False)
    fake_cols, fake_half = join(blocks, fake_cols, fake_half)
    fake_near = lax.all_to_all(fake_half, "head", 0, 0)
    mixed, packed, chances, normed, noise_term, noise_back = run(
        both_body,
        [
            ((2 * HD, L), BF),
            ((3 * HD, L), BF),
            ((L, L), F32),
            ((D, L), BF),
            ((16, F, HD), BF),
            ((HD, L), F32),
        ],
        [place],
        *blocks,
        fake_full,
        real_qkv,
        fresh,
        fake_cols,
    )
    mixed, fake_near = lax.optimization_barrier((mixed, fake_near))
    fake_far = send(fake_near, "dp", CORE)
    blocks = ring(mixed)
    fake_near, fake_far = join(blocks, fake_near, fake_far)
    keep, give = run(
        functools.partial(back_body, inv_root),
        [((8, 4 * F + HD, HD), BF), ((8, 4 * F + HD, HD), BF)],
        [place],
        *[(b, (slice(0, HD), slice(0, L))) for b in blocks],
        (gram, (slice(0, 16), slice(0, HD), slice(0, HD))),
        noise_back,
        packed,
        chances,
        (mixed, (slice(0, HD), slice(0, L))),
        noise_term,
        normed,
        scratch=[pltpu.VMEM((INNER, L), BF), pltpu.VMEM((D, 3 * HD), BF)],
    )
    give, weights = lax.optimization_barrier((give, weights))
    taken = send(give, "dp", CORE)
    gap, diff = run(
        score_body,
        [((8, HD), F32), ((L, F), F32)],
        [place],
        *blocks,
        weights,
        fake_near,
        fake_far,
        fresh_cols,
        scratch=[pltpu.VMEM((INNER, L), BF), pltpu.VMEM((F, INNER), BF)],
    )
    grad = (keep.astype(F32) + taken.astype(F32)).astype(BF)
    grad, gap = lax.optimization_barrier((grad, gap))
    got = lax.all_to_all(grad, "dp", 0, 0, axis_index_groups=CHIPS)
    for d in (1, 2, 4):
        gap = gap + send(gap, "head", along(d))
    gap, got = lax.optimization_barrier((gap, got))
    gap = gap + send(gap, "head", ACROSS)
    score_grad = (diff / (gap[0, 0] / (L * D) + 1e-05))[None]

    square = jnp.sum(got[:, 4 * F :].astype(F32), axis=0).astype(BF)
    fake_qkv_grad = jnp.concatenate(
        [jnp.sum(got[:, n * F : (n + 1) * F].astype(F32), axis=0) for n in range(3)], axis=1
    )
    (fake_out_grad,) = run(
        functools.partial(out_body, inv_root),
        [((F, HD), F32)],
        [],
        fake_rows,
        spread(square, "dp"),
        jnp.sum(got[:, 3 * F : 4 * F].astype(F32), axis=0),
    )
    return (score_grad, fake_qkv_grad, fake_out_grad)


def solution(mesh):
    in_specs = (
        P("dp", None, "head"),
        P("dp", None, None),
        P("dp"),
        P(None, "head"),
        P("head", None),
        P(None, "head"),
        P("head", None),
        P("dp", "head"),
        P("dp", "head"),
    )
    out_specs = (P("dp", None, "head"), P("dp", "head"), P("dp", "head"))
    return jax.shard_map(local, mesh=mesh, in_specs=in_specs, out_specs=out_specs, check_vma=False)
```

```python
import functools
import math

import jax
import jax.numpy as jnp
from jax import lax
from jax.experimental import pallas as pl
from jax.experimental.pallas import tpu as pltpu
from jax.sharding import PartitionSpec as P

D = 3072
HD = 128
L = 512
F = 192
Z = 8
INNER = 2048
BF = jnp.bfloat16
F32 = jnp.float32
ROOT = 1.0 / math.sqrt(HD)

HEAD = [(a, z) for a in range(2) for z in range(Z)]
ACROSS = [(a * Z + z, (1 - a) * Z + z) for a, z in HEAD]

CORE = [(i, i ^ 1) for i in range(16)]
CHIPS = [list(range(c, 16, 2)) for c in range(2)]


def along(d):
    return [(a * Z + z, a * Z + (z + d) % Z) for a, z in HEAD]


def send(v, axis, pairs):
    return lax.ppermute(v, axis, pairs)


def ring(block, wide=True):
    def up(v):
        return send(v, "head", along(1))

    def down(v):
        return send(v, "head", along(-1))

    def across(v):
        return send(v, "head", ACROSS)

    own = [block] + [None] * 7
    other = [None] * 8
    other[0] = across(block)
    own[1], own[7] = down(block), up(block)
    own[2], own[6] = down(own[1]), up(own[7])
    if wide:
        other[1], other[7] = across(own[1]), across(own[7])
    else:
        other[1], other[7] = down(other[0]), up(other[0])
    other[2], other[6] = down(other[1]), up(other[7])
    own[3], own[5] = down(own[2]), up(own[6])
    other[3], other[5] = down(other[2]), up(other[6])
    own[4] = down(own[3])
    other[4] = up(other[5])
    return own + other


def join(blocks, *arrays):
    both = lax.optimization_barrier((*blocks, *arrays))
    blocks[:] = both[:16]
    return both[16:]


def spread(block, axis):
    return lax.all_to_all(jnp.broadcast_to(block[None], (16,) + block.shape), axis, 0, 0)


def noise_levels(step):
    angle = (step.astype(F32) + 1.0) / 1001.0 * (math.pi / 2.0)
    return (jnp.cos(angle), jnp.sin(angle))


def dot(a, b, ca, cb):
    return lax.dot_general(a, b, (((ca,), (cb,)), ((), ())), preferred_element_type=F32)


class Late:
    def __init__(self, source, target, semaphore):
        self.copy = pltpu.make_async_copy(source, target, semaphore)
        self.target = target
        self.waited = False
        self.copy.start()

    def __getitem__(self, index):
        if not self.waited:
            self.copy.wait()
            self.waited = True
        return self.target[index]


def run(body, outs, scalars, *arrays, scratch=(), flops=10**9):
    cuts = [v[1] if isinstance(v, tuple) else None for v in arrays]
    arrays = [v[0] if isinstance(v, tuple) else v for v in arrays]
    shapes = [
        v.shape if c is None else tuple(s.stop - s.start for s in c)
        for v, c in zip(arrays, cuts)
    ]
    counts = [len(scalars), len(arrays), len(outs), len(arrays), len(scratch)]

    def kernel(*refs):
        groups, first = [], 0
        for count in counts:
            groups.append(refs[first : first + count])
            first += count
        numbers, sources, results, targets, spare = groups
        sources = [s if c is None else s.at[c] for s, c in zip(sources, cuts)]
        held = [Late(s, t, refs[-1].at[k]) for k, (s, t) in enumerate(zip(sources, targets))]
        body(*numbers, *held, *results, *spare)
        for late in held:
            if not late.waited:
                late.copy.wait()

    specs = [pl.BlockSpec(memory_space=pltpu.SMEM)] * len(scalars)
    specs += [pl.BlockSpec(memory_space=pl.ANY)] * len(arrays)
    return pl.pallas_call(
        kernel,
        out_shape=[jax.ShapeDtypeStruct(s, t) for s, t in outs],
        in_specs=specs,
        out_specs=[pl.BlockSpec(memory_space=pltpu.VMEM)] * len(outs),
        scratch_shapes=[
            *[pltpu.VMEM(s, v.dtype) for s, v in zip(shapes, arrays)],
            *scratch,
            pltpu.SemaphoreType.DMA((len(arrays),)),
        ],
        compiler_params=pltpu.CompilerParams(vmem_limit_bytes=56 * 1024 * 1024),
        cost_estimate=pl.CostEstimate(flops=flops, bytes_accessed=8 * 2**20, transcendentals=0),
    )(*scalars, *arrays)


def softmax_attend(packed):
    query = packed[:HD].T
    keys, values = packed[HD : 2 * HD], packed[2 * HD :]
    scores = dot(query, keys, 1, 0) * ROOT
    powers = jnp.exp(scores - jnp.max(scores, axis=1, keepdims=True))
    weights = powers / jnp.sum(powers, axis=1, keepdims=True)
    mixed = dot(values, weights.astype(BF), 1, 1).astype(BF)
    return weights, mixed


def normalize(place, blocks, normed):
    total = jnp.zeros((8, L), F32)
    for b in blocks:
        total = total + jnp.sum(b[:, :L].astype(F32).reshape(F // 8, 8, L), axis=0)
    mean = jnp.sum(total, axis=0, keepdims=True) / D
    total = jnp.zeros((8, L), F32)
    for b in blocks:
        center = b[:, :L].astype(F32) - mean
        total = total + jnp.sum((center * center).reshape(F // 8, 8, L), axis=0)
    scale = lax.rsqrt(jnp.sum(total, axis=0, keepdims=True) / D + 1e-06)
    for k, b in enumerate(blocks):
        rows = pl.ds(pl.multiple_of(place[k] * F, F), F)
        normed[rows, :] = ((b[:, :L].astype(F32) - mean) * scale).astype(BF)


def gather_slices(place, blocks, first, whole):
    for k, b in enumerate(blocks):
        for s in range(8):
            rows = pl.ds(pl.multiple_of(place[k] * 16 + s * 256, 16), 16)
            whole[rows, :] = b[first + s * 16 : first + s * 16 + 16, :]


def project_slices(which, weights, whole):
    total = jnp.zeros((F, L), F32)
    for s in range(8):
        weight = weights[2 * s + which, :, HD:]
        total = total + dot(weight, whole[s * 256 : (s + 1) * 256, :], 1, 0)
    return total


def gen_body(place, *refs):
    blocks, (weight, mixed, fake_rows, gram, normed) = refs[:16], refs[16:]
    normalize(place, blocks, normed)
    packed = dot(weight[...].T, normed[...], 1, 0).astype(BF)
    mixed[...] = softmax_attend(packed)[1]
    mine = blocks[0][:, L:].T
    for k, b in enumerate(blocks):
        part = b[:, L:]
        fake_rows[:, pl.ds(pl.multiple_of(place[k] * HD, HD), HD)] = part
        gram[place[k]] = dot(mine, part, 1, 0).astype(BF)


def both_body(place, *refs):
    blocks, refs = refs[:16], refs[16:]
    fake_weight, real_weight, fresh, columns, refs = *refs[:4], refs[4:]
    mixed, packed, weights, normed, noise_term, noise_back = refs
    normalize(place, blocks, normed)
    packed[...] = dot(fake_weight[...].T, normed[...], 1, 0).astype(BF)
    weights[...], fake_mixed = softmax_attend(packed[...])
    mixed[:HD, :] = fake_mixed
    noise_term[...] = dot(fake_mixed, fresh[...], 1, 0).T.astype(BF).reshape(16, F, HD)
    back = columns[...].reshape(D, HD).T
    noise_back[...] = dot(back, fresh[...], 1, 1)
    real_packed = dot(real_weight[...].T, normed[...], 1, 0).astype(BF)
    mixed[HD:, :] = softmax_attend(real_packed)[1]


def noised_body(place, levels, *refs):
    blocks, refs = refs[:16], refs[16:]
    weights, tokens, fresh, noised, columns, half, whole = refs
    gather_slices(place, blocks, 0, whole)
    branch = project_slices(0, weights, whole)
    generated = (tokens[...].astype(F32) + branch).astype(BF)
    noised[...] = (
        levels[0] * generated.astype(F32) + levels[1] * fresh[...].astype(F32)
    ).astype(BF)
    columns[...] = weights[:, :, :HD]
    half[...] = weights[:, pl.ds(pl.multiple_of(place[16] * (F // 2), 32), F // 2), :HD]


def back_body(inv_root, place, *refs):
    blocks, refs = refs[:16], refs[16:]
    gram, noise_back, packed, weights, mine, noise_term, normed, *refs = refs
    give, grad_packed, keep_square, whole, rows = refs
    for k, b in enumerate(blocks):
        whole[pl.ds(pl.multiple_of(place[k] * HD, HD), HD), :] = b[:HD, :]
    back = jnp.concatenate([gram[g] for g in range(16)], axis=1)
    upstream = inv_root * (dot(back, whole[...], 1, 0) - noise_back[...])
    upstream = upstream.astype(BF)
    held = packed[...]
    query, keys, values = held[:HD], held[HD : 2 * HD], held[2 * HD :]
    chances = weights[...]
    grad_weights = dot(upstream.T, values, 1, 0)
    inner = jnp.sum(grad_weights * chances, axis=1, keepdims=True)
    grad_scores = (chances * (grad_weights - inner) * ROOT).astype(BF)
    grad_values = dot(upstream, chances.astype(BF), 1, 0)
    grad_query = dot(keys, grad_scores, 1, 1)
    grad_keys = dot(query, grad_scores, 1, 0)
    grad_packed[...] = jnp.concatenate([grad_query, grad_keys, grad_values], axis=0).astype(BF)
    square = dot(whole[...], mine[:HD, :], 1, 1).astype(BF)
    whole[:, :HD] = square
    half_payload(1 - place[16], normed, grad_packed, noise_term, rows, give)
    for chip in range(8):
        for target, core in ((keep_square, place[16]), (give, 1 - place[16])):
            group = pl.ds(pl.multiple_of((2 * chip + core) * HD, HD), HD)
            last = target.shape[1] - HD
            target[chip, last:, :] = whole[group, :HD]


def half_payload(core, normed, grad_packed, noise_term, rows, target):
    for chip in range(8):
        group = 2 * chip + core
        rows[chip * F : (chip + 1) * F, :] = normed[pl.ds(pl.multiple_of(group * F, F), F), :]
    part = dot(rows[...], grad_packed[...], 1, 1).astype(BF)
    for chip in range(8):
        for n in range(3):
            piece = part[chip * F : (chip + 1) * F, n * HD : (n + 1) * HD]
            target[chip, n * F : (n + 1) * F, :] = piece
        target[chip, 3 * F : 4 * F, :] = noise_term[2 * chip + core]


def keep_body(place, grad_packed, normed, noise_term, square, keep, rows):
    half_payload(place[16], normed, grad_packed, noise_term, rows, keep)
    keep[:, 4 * F :, :] = square[...]


def score_body(place, *refs):
    blocks, refs = refs[:16], refs[16:]
    weights, near, far, fresh, gap, diff, whole, chunk = refs
    gather_slices(place, blocks, HD, whole)
    real_eps = project_slices(1, weights, whole)
    part = jnp.sum(jnp.abs(fresh[...].astype(F32) - real_eps))
    gap[...] = jnp.full((8, HD), part, F32)
    for k, b in enumerate(blocks):
        whole[pl.ds(pl.multiple_of(place[k] * HD, HD), HD), :] = b[:HD, :]
    for part, core in ((near, place[16]), (far, 1 - place[16])):
        rows = pl.ds(pl.multiple_of(core * (F // 2), 32), F // 2)
        for g in range(16):
            chunk[rows, g * HD : (g + 1) * HD] = part[g]
    fake_eps = dot(chunk[...], whole[...], 1, 0)
    diff[...] = (real_eps - fake_eps).T


def out_body(inv_root, rows, square, noise, grad):
    total = jnp.zeros((F, HD), F32)
    for g in range(16):
        total = total + dot(rows[:, g * HD : (g + 1) * HD], square[g], 1, 0)
    grad[...] = inv_root * (total - noise[...])


def local(latent, noise, steps, gen_qkv, gen_out, real_qkv, real_out, fake_qkv, fake_out):
    fresh = noise[0]
    head = lax.axis_index("head")
    dp = lax.axis_index("dp")
    a, z = head // Z, head % Z
    offsets = (z + jnp.arange(Z)) % Z
    place = jnp.concatenate([a * Z + offsets, (1 - a) * Z + offsets, dp[None] % 2])
    place = place.astype(jnp.int32)
    levels = jnp.stack(noise_levels(steps[0]))
    inv_root = 1.0 / math.sqrt(L * 16)
    fresh_cols = lax.dynamic_slice_in_dim(fresh, head * F, F, 1).T

    start = dp // 2 * 16
    rows = jnp.where(
        dp % 2 == 0,
        lax.dynamic_slice_in_dim(gen_out, start, 16, 0),
        lax.dynamic_slice_in_dim(real_out, start, 16, 0),
    )
    rows = rows.reshape(16, 16, F).transpose(1, 0, 2)
    tokens = latent[0].T
    blocks = ring(jnp.concatenate([tokens, fake_out], axis=1))
    (rows,) = join(blocks, rows)
    rows = lax.all_to_all(rows, "head", 0, 0)
    gen_mixed, fake_rows, gram = run(
        gen_body,
        [((HD, L), BF), ((F, INNER), BF), ((16, HD, HD), BF)],
        [place],
        *blocks,
        gen_qkv,
        scratch=[pltpu.VMEM((D, L), BF)],
    )
    fake_full = lax.all_gather(fake_qkv, "dp", axis=0, tiled=True)
    gen_mixed, rows = lax.optimization_barrier((gen_mixed, rows))
    rows = rows.reshape(256, F).T
    weights = lax.all_gather(jnp.concatenate([fake_out, rows], axis=1), "dp", axis=0)

    gram = lax.all_to_all(gram, "dp", 0, 0)
    blocks = ring(gen_mixed, wide=False)
    noised_part, fake_cols, fake_half = run(
        noised_body,
        [((F, L), BF), ((16, F, HD), BF), ((16, F // 2, HD), BF)],
        [place, levels],
        *blocks,
        weights,
        tokens,
        fresh_cols,
        scratch=[pltpu.VMEM((INNER, L), BF)],
    )

    noised_part, gram = lax.optimization_barrier((noised_part, gram))
    gram = jnp.sum(gram.astype(F32), axis=0).astype(BF)
    gram = lax.all_gather(jnp.pad(gram, ((0, F - HD), (0, 2 * HD))), "dp", axis=0)
    blocks = ring(noised_part, wide=False)
    fake_cols, fake_half = join(blocks, fake_cols, fake_half)
    fake_near = lax.all_to_all(fake_half, "head", 0, 0)
    mixed, packed, chances, normed, noise_term, noise_back = run(
        both_body,
        [
            ((2 * HD, L), BF),
            ((3 * HD, L), BF),
            ((L, L), F32),
            ((D, L), BF),
            ((16, F, HD), BF),
            ((HD, L), F32),
        ],
        [place],
        *blocks,
        fake_full,
        real_qkv,
        fresh,
        fake_cols,
    )
    mixed, fake_near = lax.optimization_barrier((mixed, fake_near))
    fake_far = send(fake_near, "dp", CORE)
    blocks = ring(mixed)
    fake_near, fake_far = join(blocks, fake_near, fake_far)
    give, grad_packed, square = run(
        functools.partial(back_body, inv_root),
        [((8, 4 * F + HD, HD), BF), ((3 * HD, L), BF), ((8, HD, HD), BF)],
        [place],
        *[(b, (slice(0, HD), slice(0, L))) for b in blocks],
        (gram, (slice(0, 16), slice(0, HD), slice(0, HD))),
        noise_back,
        packed,
        chances,
        (mixed, (slice(0, HD), slice(0, L))),
        noise_term,
        normed,
        scratch=[pltpu.VMEM((INNER, L), BF), pltpu.VMEM((D // 2, L), BF)],
    )
    taken = send(give, "dp", CORE)
    (keep,) = run(
        keep_body,
        [((8, 4 * F + HD, HD), BF)],
        [place],
        grad_packed,
        normed,
        noise_term,
        square,
        scratch=[pltpu.VMEM((D // 2, L), BF)],
    )
    grad = (keep.astype(F32) + taken.astype(F32)).astype(BF)
    grad, weights = lax.optimization_barrier((grad, weights))
    got = lax.all_to_all(grad, "dp", 0, 0, axis_index_groups=CHIPS)
    gap, diff = run(
        score_body,
        [((8, HD), F32), ((L, F), F32)],
        [place],
        *blocks,
        weights,
        fake_near,
        fake_far,
        fresh_cols,
        scratch=[pltpu.VMEM((INNER, L), BF), pltpu.VMEM((F, INNER), BF)],
    )
    for d in (1, 2, 4):
        gap = gap + send(gap, "head", along(d))
    gap, got = lax.optimization_barrier((gap, got))
    gap = gap + send(gap, "head", ACROSS)
    score_grad = (diff / (gap[0, 0] / (L * D) + 1e-05))[None]

    square = jnp.sum(got[:, 4 * F :].astype(F32), axis=0).astype(BF)
    fake_qkv_grad = jnp.concatenate(
        [jnp.sum(got[:, n * F : (n + 1) * F].astype(F32), axis=0) for n in range(3)], axis=1
    )
    (fake_out_grad,) = run(
        functools.partial(out_body, inv_root),
        [((F, HD), F32)],
        [],
        fake_rows,
        spread(square, "dp"),
        jnp.sum(got[:, 3 * F : 4 * F].astype(F32), axis=0),
    )
    return (score_grad, fake_qkv_grad, fake_out_grad)


def solution(mesh):
    in_specs = (
        P("dp", None, "head"),
        P("dp", None, None),
        P("dp"),
        P(None, "head"),
        P("head", None),
        P(None, "head"),
        P("head", None),
        P("dp", "head"),
        P("dp", "head"),
    )
    out_specs = (P("dp", None, "head"), P("dp", "head"), P("dp", "head"))
    return jax.shard_map(local, mesh=mesh, in_specs=in_specs, out_specs=out_specs, check_vma=False)
```

```python
import functools
import math

import jax
import jax.numpy as jnp
from jax import lax
from jax.experimental import pallas as pl
from jax.experimental.pallas import tpu as pltpu
from jax.sharding import PartitionSpec as P

D = 3072
HD = 128
L = 512
F = 192
Z = 8
INNER = 2048
BF = jnp.bfloat16
F32 = jnp.float32
ROOT = 1.0 / math.sqrt(HD)

HEAD = [(a, z) for a in range(2) for z in range(Z)]
ACROSS = [(a * Z + z, (1 - a) * Z + z) for a, z in HEAD]

CORE = [(i, i ^ 1) for i in range(16)]
CHIPS = [list(range(c, 16, 2)) for c in range(2)]


def along(d):
    return [(a * Z + z, a * Z + (z + d) % Z) for a, z in HEAD]


def send(v, axis, pairs):
    return lax.ppermute(v, axis, pairs)


def ring(block, wide=True):
    def up(v):
        return send(v, "head", along(1))

    def down(v):
        return send(v, "head", along(-1))

    def across(v):
        return send(v, "head", ACROSS)

    own = [block] + [None] * 7
    other = [None] * 8
    other[0] = across(block)
    own[1], own[7] = down(block), up(block)
    own[2], own[6] = down(own[1]), up(own[7])
    if wide:
        other[1], other[7] = across(own[1]), across(own[7])
    else:
        other[1], other[7] = down(other[0]), up(other[0])
    other[2], other[6] = down(other[1]), up(other[7])
    own[3], own[5] = down(own[2]), up(own[6])
    other[3], other[5] = down(other[2]), up(other[6])
    own[4] = down(own[3])
    other[4] = up(other[5])
    return own + other


def join(blocks, *arrays):
    both = lax.optimization_barrier((*blocks, *arrays))
    blocks[:] = both[:16]
    return both[16:]


def spread(block, axis):
    return lax.all_to_all(jnp.broadcast_to(block[None], (16,) + block.shape), axis, 0, 0)


def noise_levels(step):
    angle = (step.astype(F32) + 1.0) / 1001.0 * (math.pi / 2.0)
    return (jnp.cos(angle), jnp.sin(angle))


def dot(a, b, ca, cb):
    return lax.dot_general(a, b, (((ca,), (cb,)), ((), ())), preferred_element_type=F32)


class Late:
    def __init__(self, source, target, semaphore):
        self.copy = pltpu.make_async_copy(source, target, semaphore)
        self.target = target
        self.waited = False
        self.copy.start()

    def __getitem__(self, index):
        if not self.waited:
            self.copy.wait()
            self.waited = True
        return self.target[index]


def run(body, outs, scalars, *arrays, scratch=(), flops=10**9):
    cuts = [v[1] if isinstance(v, tuple) else None for v in arrays]
    arrays = [v[0] if isinstance(v, tuple) else v for v in arrays]
    shapes = [
        v.shape if c is None else tuple(s.stop - s.start for s in c)
        for v, c in zip(arrays, cuts)
    ]
    counts = [len(scalars), len(arrays), len(outs), len(arrays), len(scratch)]

    def kernel(*refs):
        groups, first = [], 0
        for count in counts:
            groups.append(refs[first : first + count])
            first += count
        numbers, sources, results, targets, spare = groups
        sources = [s if c is None else s.at[c] for s, c in zip(sources, cuts)]
        held = [Late(s, t, refs[-1].at[k]) for k, (s, t) in enumerate(zip(sources, targets))]
        body(*numbers, *held, *results, *spare)
        for late in held:
            if not late.waited:
                late.copy.wait()

    specs = [pl.BlockSpec(memory_space=pltpu.SMEM)] * len(scalars)
    specs += [pl.BlockSpec(memory_space=pl.ANY)] * len(arrays)
    return pl.pallas_call(
        kernel,
        out_shape=[jax.ShapeDtypeStruct(s, t) for s, t in outs],
        in_specs=specs,
        out_specs=[pl.BlockSpec(memory_space=pltpu.VMEM)] * len(outs),
        scratch_shapes=[
            *[pltpu.VMEM(s, v.dtype) for s, v in zip(shapes, arrays)],
            *scratch,
            pltpu.SemaphoreType.DMA((len(arrays),)),
        ],
        compiler_params=pltpu.CompilerParams(vmem_limit_bytes=56 * 1024 * 1024),
        cost_estimate=pl.CostEstimate(flops=flops, bytes_accessed=8 * 2**20, transcendentals=0),
    )(*scalars, *arrays)


def softmax_attend(packed):
    query = packed[:HD].T
    keys, values = packed[HD : 2 * HD], packed[2 * HD :]
    scores = dot(query, keys, 1, 0) * ROOT
    powers = jnp.exp(scores - jnp.max(scores, axis=1, keepdims=True))
    weights = powers / jnp.sum(powers, axis=1, keepdims=True)
    mixed = dot(values, weights.astype(BF), 1, 1).astype(BF)
    return weights, mixed


def normalize(place, blocks, normed):
    total = jnp.zeros((8, L), F32)
    for b in blocks:
        total = total + jnp.sum(b[:, :L].astype(F32).reshape(F // 8, 8, L), axis=0)
    mean = jnp.sum(total, axis=0, keepdims=True) / D
    total = jnp.zeros((8, L), F32)
    for b in blocks:
        center = b[:, :L].astype(F32) - mean
        total = total + jnp.sum((center * center).reshape(F // 8, 8, L), axis=0)
    scale = lax.rsqrt(jnp.sum(total, axis=0, keepdims=True) / D + 1e-06)
    for k, b in enumerate(blocks):
        rows = pl.ds(pl.multiple_of(place[k] * F, F), F)
        normed[rows, :] = ((b[:, :L].astype(F32) - mean) * scale).astype(BF)


def gather_slices(place, blocks, first, whole):
    for k, b in enumerate(blocks):
        for s in range(8):
            rows = pl.ds(pl.multiple_of(place[k] * 16 + s * 256, 16), 16)
            whole[rows, :] = b[first + s * 16 : first + s * 16 + 16, :]


def project_slices(which, weights, whole):
    total = jnp.zeros((F, L), F32)
    for s in range(8):
        weight = weights[2 * s + which, :, HD:]
        total = total + dot(weight, whole[s * 256 : (s + 1) * 256, :], 1, 0)
    return total


def gen_body(place, *refs):
    blocks, (weight, mixed, fake_rows, gram, normed) = refs[:16], refs[16:]
    normalize(place, blocks, normed)
    packed = dot(weight[...].T, normed[...], 1, 0).astype(BF)
    mixed[...] = softmax_attend(packed)[1]
    mine = blocks[0][:, L:].T
    for k, b in enumerate(blocks):
        part = b[:, L:]
        fake_rows[:, pl.ds(pl.multiple_of(place[k] * HD, HD), HD)] = part
        gram[place[k]] = dot(mine, part, 1, 0).astype(BF)


def both_body(place, *refs):
    blocks, refs = refs[:16], refs[16:]
    fake_weight, real_weight, fresh, columns, refs = *refs[:4], refs[4:]
    mixed, packed, weights, normed, noise_term, noise_back = refs
    normalize(place, blocks, normed)
    packed[...] = dot(fake_weight[...].T, normed[...], 1, 0).astype(BF)
    weights[...], fake_mixed = softmax_attend(packed[...])
    mixed[:HD, :] = fake_mixed
    noise_term[...] = dot(fake_mixed, fresh[...], 1, 0).T.astype(BF).reshape(16, F, HD)
    back = columns[...].reshape(D, HD).T
    noise_back[...] = dot(back, fresh[...], 1, 1)
    real_packed = dot(real_weight[...].T, normed[...], 1, 0).astype(BF)
    mixed[HD:, :] = softmax_attend(real_packed)[1]


def noised_body(place, levels, *refs):
    blocks, refs = refs[:16], refs[16:]
    weights, tokens, fresh, noised, columns, half, whole = refs
    gather_slices(place, blocks, 0, whole)
    branch = project_slices(0, weights, whole)
    generated = (tokens[...].astype(F32) + branch).astype(BF)
    noised[...] = (
        levels[0] * generated.astype(F32) + levels[1] * fresh[...].astype(F32)
    ).astype(BF)
    columns[...] = weights[:, :, :HD]
    half[...] = weights[:, pl.ds(pl.multiple_of(place[16] * (F // 2), 32), F // 2), :HD]


def back_body(inv_root, place, *refs):
    blocks, refs = refs[:16], refs[16:]
    gram, noise_back, packed, weights, mine, noise_term, normed, *refs = refs
    give, grad_packed, keep_square, whole, rows = refs
    for k, b in enumerate(blocks):
        whole[pl.ds(pl.multiple_of(place[k] * HD, HD), HD), :] = b[:HD, :]
    back = jnp.concatenate([gram[g] for g in range(16)], axis=1)
    upstream = inv_root * (dot(back, whole[...], 1, 0) - noise_back[...])
    upstream = upstream.astype(BF)
    held = packed[...]
    query, keys, values = held[:HD], held[HD : 2 * HD], held[2 * HD :]
    chances = weights[...]
    grad_weights = dot(upstream.T, values, 1, 0)
    inner = jnp.sum(grad_weights * chances, axis=1, keepdims=True)
    grad_scores = (chances * (grad_weights - inner) * ROOT).astype(BF)
    grad_values = dot(upstream, chances.astype(BF), 1, 0)
    grad_query = dot(keys, grad_scores, 1, 1)
    grad_keys = dot(query, grad_scores, 1, 0)
    grad_packed[...] = jnp.concatenate([grad_query, grad_keys, grad_values], axis=0).astype(BF)
    square = dot(whole[...], mine[:HD, :], 1, 1).astype(BF)
    whole[:, :HD] = square
    half_payload(1 - place[16], normed, grad_packed, noise_term, rows, give)
    for chip in range(8):
        for target, core in ((keep_square, place[16]), (give, 1 - place[16])):
            group = pl.ds(pl.multiple_of((2 * chip + core) * HD, HD), HD)
            last = target.shape[1] - HD
            target[chip, last:, :] = whole[group, :HD]


def half_payload(core, normed, grad_packed, noise_term, rows, target):
    for chip in range(8):
        group = 2 * chip + core
        rows[chip * F : (chip + 1) * F, :] = normed[pl.ds(pl.multiple_of(group * F, F), F), :]
    part = dot(rows[...], grad_packed[...], 1, 1).astype(BF)
    for chip in range(8):
        for n in range(3):
            piece = part[chip * F : (chip + 1) * F, n * HD : (n + 1) * HD]
            target[chip, n * F : (n + 1) * F, :] = piece
        target[chip, 3 * F : 4 * F, :] = noise_term[2 * chip + core]


def keep_body(place, grad_packed, normed, noise_term, square, keep, rows):
    half_payload(place[16], normed, grad_packed, noise_term, rows, keep)
    keep[:, 4 * F :, :] = square[...]


def score_body(place, *refs):
    blocks, refs = refs[:16], refs[16:]
    weights, near, far, fresh, gap, diff, whole, chunk = refs
    gather_slices(place, blocks, HD, whole)
    real_eps = project_slices(1, weights, whole)
    part = jnp.sum(jnp.abs(fresh[...].astype(F32) - real_eps))
    gap[...] = jnp.full((8, HD), part, F32)
    for k, b in enumerate(blocks):
        whole[pl.ds(pl.multiple_of(place[k] * HD, HD), HD), :] = b[:HD, :]
    for part, core in ((near, place[16]), (far, 1 - place[16])):
        rows = pl.ds(pl.multiple_of(core * (F // 2), 32), F // 2)
        for g in range(16):
            chunk[rows, g * HD : (g + 1) * HD] = part[g]
    fake_eps = dot(chunk[...], whole[...], 1, 0)
    diff[...] = (real_eps - fake_eps).T


def out_body(inv_root, rows, square, noise, grad):
    total = jnp.zeros((F, HD), F32)
    for g in range(16):
        total = total + dot(rows[:, g * HD : (g + 1) * HD], square[g], 1, 0)
    grad[...] = inv_root * (total - noise[...])


def local(latent, noise, steps, gen_qkv, gen_out, real_qkv, real_out, fake_qkv, fake_out):
    fresh = noise[0]
    head = lax.axis_index("head")
    dp = lax.axis_index("dp")
    a, z = head // Z, head % Z
    offsets = (z + jnp.arange(Z)) % Z
    place = jnp.concatenate([a * Z + offsets, (1 - a) * Z + offsets, dp[None] % 2])
    place = place.astype(jnp.int32)
    levels = jnp.stack(noise_levels(steps[0]))
    inv_root = 1.0 / math.sqrt(L * 16)
    fresh_cols = lax.dynamic_slice_in_dim(fresh, head * F, F, 1).T

    start = dp // 2 * 16
    rows = jnp.where(
        dp % 2 == 0,
        lax.dynamic_slice_in_dim(gen_out, start, 16, 0),
        lax.dynamic_slice_in_dim(real_out, start, 16, 0),
    )
    rows = rows.reshape(16, 16, F).transpose(1, 0, 2)
    tokens = latent[0].T
    blocks = ring(jnp.concatenate([tokens, fake_out], axis=1))
    (rows,) = join(blocks, rows)
    rows = lax.all_to_all(rows, "head", 0, 0)
    gen_mixed, fake_rows, gram = run(
        gen_body,
        [((HD, L), BF), ((F, INNER), BF), ((16, HD, HD), BF)],
        [place],
        *blocks,
        gen_qkv,
        scratch=[pltpu.VMEM((D, L), BF)],
    )
    fake_full = lax.all_gather(fake_qkv, "dp", axis=0, tiled=True)
    gen_mixed, rows = lax.optimization_barrier((gen_mixed, rows))
    rows = rows.reshape(256, F).T
    weights = lax.all_gather(jnp.concatenate([fake_out, rows], axis=1), "dp", axis=0)

    gram = lax.all_to_all(gram, "dp", 0, 0)
    blocks = ring(gen_mixed, wide=False)
    noised_part, fake_cols, fake_half = run(
        noised_body,
        [((F, L), BF), ((16, F, HD), BF), ((16, F // 2, HD), BF)],
        [place, levels],
        *blocks,
        weights,
        tokens,
        fresh_cols,
        scratch=[pltpu.VMEM((INNER, L), BF)],
    )

    noised_part, gram = lax.optimization_barrier((noised_part, gram))
    gram = jnp.sum(gram.astype(F32), axis=0).astype(BF)
    gram = lax.all_gather(jnp.pad(gram, ((0, F - HD), (0, 2 * HD))), "dp", axis=0)
    blocks = ring(noised_part, wide=False)
    fake_cols, fake_half = join(blocks, fake_cols, fake_half)
    fake_near = lax.all_to_all(fake_half, "head", 0, 0)
    mixed, packed, chances, normed, noise_term, noise_back = run(
        both_body,
        [
            ((2 * HD, L), BF),
            ((3 * HD, L), BF),
            ((L, L), F32),
            ((D, L), BF),
            ((16, F, HD), BF),
            ((HD, L), F32),
        ],
        [place],
        *blocks,
        fake_full,
        real_qkv,
        fresh,
        fake_cols,
    )
    mixed, fake_near = lax.optimization_barrier((mixed, fake_near))
    fake_far = send(fake_near, "dp", CORE)
    blocks = ring(mixed)
    fake_near, fake_far = join(blocks, fake_near, fake_far)
    give, grad_packed, square = run(
        functools.partial(back_body, inv_root),
        [((8, 4 * F + HD, HD), BF), ((3 * HD, L), BF), ((8, HD, HD), BF)],
        [place],
        *[(b, (slice(0, HD), slice(0, L))) for b in blocks],
        (gram, (slice(0, 16), slice(0, HD), slice(0, HD))),
        noise_back,
        packed,
        chances,
        (mixed, (slice(0, HD), slice(0, L))),
        noise_term,
        normed,
        scratch=[pltpu.VMEM((INNER, L), BF), pltpu.VMEM((D // 2, L), BF)],
    )
    taken = send(give, "dp", CORE)
    (keep,) = run(
        keep_body,
        [((8, 4 * F + HD, HD), BF)],
        [place],
        grad_packed,
        normed,
        noise_term,
        square,
        scratch=[pltpu.VMEM((D // 2, L), BF)],
    )
    grad = (keep.astype(F32) + taken.astype(F32)).astype(BF)
    grad, weights = lax.optimization_barrier((grad, weights))
    got = lax.all_to_all(grad, "dp", 0, 0, axis_index_groups=CHIPS)
    gap, diff = run(
        score_body,
        [((8, HD), F32), ((L, F), F32)],
        [place],
        *blocks,
        weights,
        fake_near,
        fake_far,
        fresh_cols,
        scratch=[pltpu.VMEM((INNER, L), BF), pltpu.VMEM((F, INNER), BF)],
    )
    for d in (1, 2):
        gap = gap + send(gap, "head", along(d))
    gap, got = lax.optimization_barrier((gap, got))
    gap = gap + send(gap, "head", along(4))
    gap = gap + send(gap, "head", ACROSS)
    score_grad = (diff / (gap[0, 0] / (L * D) + 1e-05))[None]

    square = jnp.sum(got[:, 4 * F :].astype(F32), axis=0).astype(BF)
    fake_qkv_grad = jnp.concatenate(
        [jnp.sum(got[:, n * F : (n + 1) * F].astype(F32), axis=0) for n in range(3)], axis=1
    )
    (fake_out_grad,) = run(
        functools.partial(out_body, inv_root),
        [((F, HD), F32)],
        [],
        fake_rows,
        spread(square, "dp"),
        jnp.sum(got[:, 3 * F : 4 * F].astype(F32), axis=0),
    )
    return (score_grad, fake_qkv_grad, fake_out_grad)


def solution(mesh):
    in_specs = (
        P("dp", None, "head"),
        P("dp", None, None),
        P("dp"),
        P(None, "head"),
        P("head", None),
        P(None, "head"),
        P("head", None),
        P("dp", "head"),
        P("dp", "head"),
    )
    out_specs = (P("dp", None, "head"), P("dp", "head"), P("dp", "head"))
    return jax.shard_map(local, mesh=mesh, in_specs=in_specs, out_specs=out_specs, check_vma=False)
```

```python
import functools
import math

import jax
import jax.numpy as jnp
from jax import lax
from jax.experimental import pallas as pl
from jax.experimental.pallas import tpu as pltpu
from jax.sharding import PartitionSpec as P

D = 3072
HD = 128
L = 512
F = 192
Z = 8
INNER = 2048
BF = jnp.bfloat16
F32 = jnp.float32
ROOT = 1.0 / math.sqrt(HD)

HEAD = [(a, z) for a in range(2) for z in range(Z)]
ACROSS = [(a * Z + z, (1 - a) * Z + z) for a, z in HEAD]

ACROSS_FAR = [(a * Z + z, (1 - a) * Z + (z + 4) % Z) for a, z in HEAD]
CORE = [(i, i ^ 1) for i in range(16)]
CHIPS = [list(range(c, 16, 2)) for c in range(2)]


def along(d):
    return [(a * Z + z, a * Z + (z + d) % Z) for a, z in HEAD]


def send(v, axis, pairs):
    return lax.ppermute(v, axis, pairs)


def ring(block, wide=1):
    def up(v):
        return send(v, "head", along(1))

    def down(v):
        return send(v, "head", along(-1))

    def across(v):
        return send(v, "head", ACROSS)

    own = [block] + [None] * 7
    other = [None] * 8
    other[0] = across(block)
    own[1], own[7] = down(block), up(block)
    own[2], own[6] = down(own[1]), up(own[7])
    if wide:
        other[1], other[7] = across(own[1]), across(own[7])
    else:
        other[1], other[7] = down(other[0]), up(other[0])
    if wide > 1:
        other[2], other[6] = across(own[2]), across(own[6])
    else:
        other[2], other[6] = down(other[1]), up(other[7])
    own[3], own[5] = down(own[2]), up(own[6])
    other[3], other[5] = down(other[2]), up(other[6])
    own[4] = down(own[3])
    other[4] = up(other[5])
    return own + other


def join(blocks, *arrays):
    both = lax.optimization_barrier((*blocks, *arrays))
    blocks[:] = both[:16]
    return both[16:]


def spread(block, axis):
    return lax.all_to_all(jnp.broadcast_to(block[None], (16,) + block.shape), axis, 0, 0)


def noise_levels(step):
    angle = (step.astype(F32) + 1.0) / 1001.0 * (math.pi / 2.0)
    return (jnp.cos(angle), jnp.sin(angle))


def dot(a, b, ca, cb):
    return lax.dot_general(a, b, (((ca,), (cb,)), ((), ())), preferred_element_type=F32)


class Late:
    def __init__(self, source, target, semaphore):
        self.copy = pltpu.make_async_copy(source, target, semaphore)
        self.target = target
        self.waited = False
        self.copy.start()

    def __getitem__(self, index):
        if not self.waited:
            self.copy.wait()
            self.waited = True
        return self.target[index]


def run(body, outs, scalars, *arrays, scratch=(), flops=10**9):
    cuts = [v[1] if isinstance(v, tuple) else None for v in arrays]
    arrays = [v[0] if isinstance(v, tuple) else v for v in arrays]
    shapes = [
        v.shape if c is None else tuple(s.stop - s.start for s in c)
        for v, c in zip(arrays, cuts)
    ]
    counts = [len(scalars), len(arrays), len(outs), len(arrays), len(scratch)]

    def kernel(*refs):
        groups, first = [], 0
        for count in counts:
            groups.append(refs[first : first + count])
            first += count
        numbers, sources, results, targets, spare = groups
        sources = [s if c is None else s.at[c] for s, c in zip(sources, cuts)]
        held = [Late(s, t, refs[-1].at[k]) for k, (s, t) in enumerate(zip(sources, targets))]
        body(*numbers, *held, *results, *spare)
        for late in held:
            if not late.waited:
                late.copy.wait()

    specs = [pl.BlockSpec(memory_space=pltpu.SMEM)] * len(scalars)
    specs += [pl.BlockSpec(memory_space=pl.ANY)] * len(arrays)
    return pl.pallas_call(
        kernel,
        out_shape=[jax.ShapeDtypeStruct(s, t) for s, t in outs],
        in_specs=specs,
        out_specs=[pl.BlockSpec(memory_space=pltpu.VMEM)] * len(outs),
        scratch_shapes=[
            *[pltpu.VMEM(s, v.dtype) for s, v in zip(shapes, arrays)],
            *scratch,
            pltpu.SemaphoreType.DMA((len(arrays),)),
        ],
        compiler_params=pltpu.CompilerParams(vmem_limit_bytes=56 * 1024 * 1024),
        cost_estimate=pl.CostEstimate(flops=flops, bytes_accessed=8 * 2**20, transcendentals=0),
    )(*scalars, *arrays)


def softmax_attend(packed):
    query = packed[:HD].T
    keys, values = packed[HD : 2 * HD], packed[2 * HD :]
    scores = dot(query, keys, 1, 0) * ROOT
    powers = jnp.exp(scores - jnp.max(scores, axis=1, keepdims=True))
    weights = powers / jnp.sum(powers, axis=1, keepdims=True)
    mixed = dot(values, weights.astype(BF), 1, 1).astype(BF)
    return weights, mixed


def normalize(place, blocks, normed):
    total = jnp.zeros((8, L), F32)
    for b in blocks:
        total = total + jnp.sum(b[:, :L].astype(F32).reshape(F // 8, 8, L), axis=0)
    mean = jnp.sum(total, axis=0, keepdims=True) / D
    total = jnp.zeros((8, L), F32)
    for b in blocks:
        center = b[:, :L].astype(F32) - mean
        total = total + jnp.sum((center * center).reshape(F // 8, 8, L), axis=0)
    scale = lax.rsqrt(jnp.sum(total, axis=0, keepdims=True) / D + 1e-06)
    for k, b in enumerate(blocks):
        rows = pl.ds(pl.multiple_of(place[k] * F, F), F)
        normed[rows, :] = ((b[:, :L].astype(F32) - mean) * scale).astype(BF)


def gather_slices(place, blocks, first, whole):
    for k, b in enumerate(blocks):
        for s in range(8):
            rows = pl.ds(pl.multiple_of(place[k] * 16 + s * 256, 16), 16)
            whole[rows, :] = b[first + s * 16 : first + s * 16 + 16, :]


def project_slices(which, weights, whole):
    total = jnp.zeros((F, L), F32)
    for s in range(8):
        weight = weights[2 * s + which, :, HD:]
        total = total + dot(weight, whole[s * 256 : (s + 1) * 256, :], 1, 0)
    return total


def gen_body(place, *refs):
    blocks, (weight, mixed, fake_rows, gram, normed) = refs[:16], refs[16:]
    normalize(place, blocks, normed)
    packed = dot(weight[...].T, normed[...], 1, 0).astype(BF)
    mixed[...] = softmax_attend(packed)[1]
    mine = blocks[0][:, L:].T
    for k, b in enumerate(blocks):
        part = b[:, L:]
        fake_rows[:, pl.ds(pl.multiple_of(place[k] * HD, HD), HD)] = part
        gram[place[k]] = dot(mine, part, 1, 0).astype(BF)


def both_body(place, *refs):
    blocks, refs = refs[:16], refs[16:]
    fake_weight, real_weight, fresh, columns, refs = *refs[:4], refs[4:]
    mixed, packed, weights, normed, noise_term, noise_back = refs
    normalize(place, blocks, normed)
    packed[...] = dot(fake_weight[...].T, normed[...], 1, 0).astype(BF)
    weights[...], fake_mixed = softmax_attend(packed[...])
    mixed[:HD, :] = fake_mixed
    noise_term[...] = dot(fake_mixed, fresh[...], 1, 0).T.astype(BF).reshape(16, F, HD)
    back = columns[...].reshape(D, HD).T
    noise_back[...] = dot(back, fresh[...], 1, 1)
    real_packed = dot(real_weight[...].T, normed[...], 1, 0).astype(BF)
    mixed[HD:, :] = softmax_attend(real_packed)[1]


def noised_body(place, levels, *refs):
    blocks, refs = refs[:16], refs[16:]
    weights, tokens, fresh, noised, columns, half, whole = refs
    gather_slices(place, blocks, 0, whole)
    branch = project_slices(0, weights, whole)
    generated = (tokens[...].astype(F32) + branch).astype(BF)
    noised[...] = (
        levels[0] * generated.astype(F32) + levels[1] * fresh[...].astype(F32)
    ).astype(BF)
    columns[...] = weights[:, :, :HD]
    half[...] = weights[:, pl.ds(pl.multiple_of(place[16] * (F // 2), 32), F // 2), :HD]


def back_body(inv_root, place, *refs):
    blocks, refs = refs[:16], refs[16:]
    gram, noise_back, packed, weights, mine, noise_term, normed, keep, give, whole, rows = refs
    for k, b in enumerate(blocks):
        whole[pl.ds(pl.multiple_of(place[k] * HD, HD), HD), :] = b[:HD, :]
    back = jnp.concatenate([gram[g] for g in range(16)], axis=1)
    upstream = inv_root * (dot(back, whole[...], 1, 0) - noise_back[...])
    upstream = upstream.astype(BF)
    held = packed[...]
    query, keys, values = held[:HD], held[HD : 2 * HD], held[2 * HD :]
    chances = weights[...]
    grad_weights = dot(upstream.T, values, 1, 0)
    inner = jnp.sum(grad_weights * chances, axis=1, keepdims=True)
    grad_scores = (chances * (grad_weights - inner) * ROOT).astype(BF)
    grad_values = dot(upstream, chances.astype(BF), 1, 0)
    grad_query = dot(keys, grad_scores, 1, 1)
    grad_keys = dot(query, grad_scores, 1, 0)
    grad_packed = jnp.concatenate([grad_query, grad_keys, grad_values], axis=0).astype(BF)
    rows[...] = dot(normed[...], grad_packed, 1, 1).astype(BF)
    square = dot(whole[...], mine[:HD, :], 1, 1).astype(BF)
    whole[:, :HD] = square
    for chip in range(8):
        for target, core in ((keep, place[16]), (give, 1 - place[16])):
            group = 2 * chip + core
            part = rows[pl.ds(pl.multiple_of(group * F, F), F), :]
            for n in range(3):
                target[chip, n * F : (n + 1) * F, :] = part[:, n * HD : (n + 1) * HD]
            target[chip, 3 * F : 4 * F, :] = noise_term[group]
            target[chip, 4 * F :, :] = whole[pl.ds(pl.multiple_of(group * HD, HD), HD), :HD]


def score_body(place, *refs):
    blocks, refs = refs[:16], refs[16:]
    weights, near, far, fresh, gap, diff, whole, chunk = refs
    gather_slices(place, blocks, HD, whole)
    real_eps = project_slices(1, weights, whole)
    part = jnp.sum(jnp.abs(fresh[...].astype(F32) - real_eps))
    gap[...] = jnp.full((8, HD), part, F32)
    for k, b in enumerate(blocks):
        whole[pl.ds(pl.multiple_of(place[k] * HD, HD), HD), :] = b[:HD, :]
    for part, core in ((near, place[16]), (far, 1 - place[16])):
        rows = pl.ds(pl.multiple_of(core * (F // 2), 32), F // 2)
        for g in range(16):
            chunk[rows, g * HD : (g + 1) * HD] = part[g]
    fake_eps = dot(chunk[...], whole[...], 1, 0)
    diff[...] = (real_eps - fake_eps).T


def out_body(inv_root, rows, square, noise, grad):
    total = jnp.zeros((F, HD), F32)
    for g in range(16):
        total = total + dot(rows[:, g * HD : (g + 1) * HD], square[g], 1, 0)
    grad[...] = inv_root * (total - noise[...])


def local(latent, noise, steps, gen_qkv, gen_out, real_qkv, real_out, fake_qkv, fake_out):
    fresh = noise[0]
    head = lax.axis_index("head")
    dp = lax.axis_index("dp")
    a, z = head // Z, head % Z
    offsets = (z + jnp.arange(Z)) % Z
    place = jnp.concatenate([a * Z + offsets, (1 - a) * Z + offsets, dp[None] % 2])
    place = place.astype(jnp.int32)
    levels = jnp.stack(noise_levels(steps[0]))
    inv_root = 1.0 / math.sqrt(L * 16)
    fresh_cols = lax.dynamic_slice_in_dim(fresh, head * F, F, 1).T

    start = dp // 2 * 16
    rows = jnp.where(
        dp % 2 == 0,
        lax.dynamic_slice_in_dim(gen_out, start, 16, 0),
        lax.dynamic_slice_in_dim(real_out, start, 16, 0),
    )
    rows = rows.reshape(16, 16, F).transpose(1, 0, 2)
    tokens = latent[0].T
    blocks = ring(jnp.concatenate([tokens, fake_out], axis=1))
    (rows,) = join(blocks, rows)
    rows = lax.all_to_all(rows, "head", 0, 0)
    gen_mixed, fake_rows, gram = run(
        gen_body,
        [((HD, L), BF), ((F, INNER), BF), ((16, HD, HD), BF)],
        [place],
        *blocks,
        gen_qkv,
        scratch=[pltpu.VMEM((D, L), BF)],
    )
    fake_full = lax.all_gather(fake_qkv, "dp", axis=0, tiled=True)
    gen_mixed, rows = lax.optimization_barrier((gen_mixed, rows))
    rows = rows.reshape(256, F).T
    weights = lax.all_gather(jnp.concatenate([fake_out, rows], axis=1), "dp", axis=0)

    gram = lax.all_to_all(gram, "dp", 0, 0)
    blocks = ring(gen_mixed, wide=0)
    noised_part, fake_cols, fake_half = run(
        noised_body,
        [((F, L), BF), ((16, F, HD), BF), ((16, F // 2, HD), BF)],
        [place, levels],
        *blocks,
        weights,
        tokens,
        fresh_cols,
        scratch=[pltpu.VMEM((INNER, L), BF)],
    )

    noised_part, gram = lax.optimization_barrier((noised_part, gram))
    gram = jnp.sum(gram.astype(F32), axis=0).astype(BF)
    gram = lax.all_gather(jnp.pad(gram, ((0, F - HD), (0, 2 * HD))), "dp", axis=0)
    blocks = ring(noised_part, wide=0)
    fake_cols, fake_half = join(blocks, fake_cols, fake_half)
    fake_near = lax.all_to_all(fake_half, "head", 0, 0)
    mixed, packed, chances, normed, noise_term, noise_back = run(
        both_body,
        [
            ((2 * HD, L), BF),
            ((3 * HD, L), BF),
            ((L, L), F32),
            ((D, L), BF),
            ((16, F, HD), BF),
            ((HD, L), F32),
        ],
        [place],
        *blocks,
        fake_full,
        real_qkv,
        fresh,
        fake_cols,
    )
    mixed, fake_near = lax.optimization_barrier((mixed, fake_near))
    fake_far = send(fake_near, "dp", CORE)
    blocks = ring(mixed)
    fake_near, fake_far = join(blocks, fake_near, fake_far)
    keep, give = run(
        functools.partial(back_body, inv_root),
        [((8, 4 * F + HD, HD), BF), ((8, 4 * F + HD, HD), BF)],
        [place],
        *[(b, (slice(0, HD), slice(0, L))) for b in blocks],
        (gram, (slice(0, 16), slice(0, HD), slice(0, HD))),
        noise_back,
        packed,
        chances,
        (mixed, (slice(0, HD), slice(0, L))),
        noise_term,
        normed,
        scratch=[pltpu.VMEM((INNER, L), BF), pltpu.VMEM((D, 3 * HD), BF)],
    )
    give, weights = lax.optimization_barrier((give, weights))
    taken = send(give, "dp", CORE)
    gap, diff = run(
        score_body,
        [((8, HD), F32), ((L, F), F32)],
        [place],
        *blocks,
        weights,
        fake_near,
        fake_far,
        fresh_cols,
        scratch=[pltpu.VMEM((INNER, L), BF), pltpu.VMEM((F, INNER), BF)],
    )
    grad = (keep.astype(F32) + taken.astype(F32)).astype(BF)
    grad, gap = lax.optimization_barrier((grad, gap))
    got = lax.all_to_all(grad, "dp", 0, 0, axis_index_groups=CHIPS)
    gap = gap + sum(send(gap, "head", along(d)) for d in (1, 2, 3))
    gap = gap + sum(send(gap, "head", p) for p in (along(4), ACROSS, ACROSS_FAR))
    score_grad = (diff / (gap[0, 0] / (L * D) + 1e-05))[None]

    square = jnp.sum(got[:, 4 * F :].astype(F32), axis=0).astype(BF)
    fake_qkv_grad = jnp.concatenate(
        [jnp.sum(got[:, n * F : (n + 1) * F].astype(F32), axis=0) for n in range(3)], axis=1
    )
    (fake_out_grad,) = run(
        functools.partial(out_body, inv_root),
        [((F, HD), F32)],
        [],
        fake_rows,
        spread(square, "dp"),
        jnp.sum(got[:, 3 * F : 4 * F].astype(F32), axis=0),
    )
    return (score_grad, fake_qkv_grad, fake_out_grad)


def solution(mesh):
    in_specs = (
        P("dp", None, "head"),
        P("dp", None, None),
        P("dp"),
        P(None, "head"),
        P("head", None),
        P(None, "head"),
        P("head", None),
        P("dp", "head"),
        P("dp", "head"),
    )
    out_specs = (P("dp", None, "head"), P("dp", "head"), P("dp", "head"))
    return jax.shard_map(local, mesh=mesh, in_specs=in_specs, out_specs=out_specs, check_vma=False)
```
